32 devices in a mesh: shard: 8 (over z, x), tensor: 4 (over y, core).
Axes of the slice: x: 2, y: 2, z: 4, core: 2. Of those that a mesh axis runs over, the one named last changes fastest.
Arguments:
- gradients: bfloat16 [8, 1152, 1152], P(None, 'shard', 'tensor')
- weights: float32 [8, 1152, 1152], P(None, 'shard', 'tensor'), may hold values from -0.1875 to 0.1875
- owner_list: int32 [8], replicated, may hold values from 0 to 7, as said below
- left_gram_stats: float32 [16, 1152, 1152], P('shard', 'tensor'), may hold values from -6 to 6
- right_gram_stats: float32 [16, 1152, 1152], P('shard', 'tensor'), may hold values from -6 to 6
- left_root: bfloat16 [16, 1152, 1152], P('shard', None, 'tensor'), as said below
- right_root: bfloat16 [16, 1152, 1152], P('shard', None, 'tensor'), as said below
- adam_second_moment: float32 [16, 1152, 1152], P('shard', None, 'tensor'), may hold values from 0.1 to 10
Outputs:
- new_weights: float32 [8, 1152, 1152], P(None, 'shard', 'tensor')
- new_left: float32 [16, 1152, 1152], P('shard', 'tensor')
- new_right: float32 [16, 1152, 1152], P('shard', 'tensor')
- new_moment: float32 [16, 1152, 1152], P('shard', None, 'tensor')
The draws below stay inside these ranges and needn't reach their ends.
Inputs may be any that keep to these rules, and one draw needn't show every extreme that they name: `owner_list`: each owner index is named by at most 2 blocks, and some index by exactly 2. `left_root`: each slot's matrix is symmetric. `right_root`: each slot's matrix is symmetric.
All inputs are finite; a program needn't handle non-finite values.
Results may differ from the reference program's by a relative error of at most 0.0022.
Values may be sent and summed in bfloat16 or wider, within the bound.
A program may use at most 128 MiB of HBM per device.

```python
import math
import jax
import jax.numpy as jnp
from jax import lax

MODEL_WIDTH = 1152
SLOTS = 2
NB = 8
SLOT_TOTAL = 16


def draw_gradients(key, part):
    key_noise = jax.random.fold_in(key, 11)
    key_rows = jax.random.fold_in(key, 12)
    key_cols = jax.random.fold_in(key, 13)
    random_noise = jnp.clip(jax.random.normal(key_noise, (NB, MODEL_WIDTH, MODEL_WIDTH), jnp.float32), -4.0, 4.0)
    ramp_top = 3.0
    row_scale = jnp.exp(jax.random.uniform(key_rows, (NB, MODEL_WIDTH, 1), jnp.float32, jnp.log(0.3), jnp.log(3.0)))
    col_scale = jnp.exp(jax.random.uniform(key_cols, (NB, 1, MODEL_WIDTH), jnp.float32, jnp.log(0.5), jnp.log(2.0)))
    column_place = jnp.arange(MODEL_WIDTH, dtype=jnp.float32) / (MODEL_WIDTH - 1.0)
    column_ramp = jnp.exp(column_place * jnp.log(ramp_top))[None, None, :] / ramp_top ** 0.5
    return (random_noise * row_scale * col_scale * column_ramp).astype(jnp.bfloat16)


def draw_owner_list(key, part):
    key_perm = jax.random.fold_in(key, 21)
    key_coin = jax.random.fold_in(key, 22)
    key_order = jax.random.fold_in(key, 23)
    shuffled = jax.random.permutation(key_perm, NB).astype(jnp.int32)
    coins = jax.random.randint(key_coin, (NB // 2,), 0, 2).astype(jnp.int32)
    coins = coins.at[0].set(1)
    positions = jnp.arange(NB, dtype=jnp.int32)
    pair_index = positions // 2
    first_owner = shuffled[2 * pair_index]
    second_owner = shuffled[2 * pair_index + 1]
    odd_place = positions % 2
    chosen = jnp.where(odd_place == 0, first_owner, jnp.where(coins[pair_index] == 1, first_owner, second_owner))
    order = jax.random.permutation(key_order, NB).astype(jnp.int32)
    return jnp.zeros((NB,), jnp.int32).at[order].set(chosen)


def root_matrix(key):
    key_offdiagonal = jax.random.fold_in(key, 31)
    key_diagonal = jax.random.fold_in(key, 32)
    random_noise = jnp.clip(jax.random.normal(key_offdiagonal, (SLOT_TOTAL, MODEL_WIDTH, MODEL_WIDTH), jnp.float32), -5.0, 5.0)
    symmetric = (random_noise + jnp.transpose(random_noise, (0, 2, 1))) * (0.3 / (2.0 * MODEL_WIDTH) ** 0.5)
    diagonal_entries = jnp.exp(jax.random.uniform(key_diagonal, (SLOT_TOTAL, 1, MODEL_WIDTH), jnp.float32, 0.0, jnp.log(3.0)))
    eye_mask = jnp.eye(MODEL_WIDTH, dtype=jnp.bool_)[None, :, :]
    return jnp.where(eye_mask, diagonal_entries, symmetric).astype(jnp.bfloat16)


def draw_left_root(key, part):
    return root_matrix(jax.random.fold_in(key, 41))


def draw_right_root(key, part):
    return root_matrix(jax.random.fold_in(key, 42))


def block_scale(stream_key, dims, split, least, high):
    def one(axis_at, blocks):
        steps = jax.random.uniform(jax.random.fold_in(jax.random.fold_in(stream_key, 6), axis_at), (blocks,), jnp.float32, least / len(split), high / len(split))
        return jnp.repeat(jnp.exp(steps), dims[axis_at] // blocks).reshape((-1,) + (1,) * (len(dims) - axis_at - 1))

    loudness = one(*split[0])
    for cut in split[1:]:
        loudness = loudness * one(*cut)
    return loudness


def gaussian(key, dims, deviation, most, split=(), kind=jnp.bfloat16):
    factor_of = block_scale(key, dims, split, -0.22, 0.18) if split else 1.0
    entries = jax.random.normal(key, dims, jnp.float32) * deviation * factor_of
    return jnp.minimum(jnp.maximum(entries, -most), most).astype(kind)


def setup_inputs(seed: int = 0) -> dict:
    keys = jax.random.split(jax.random.key(seed), 9)
    gradients = draw_gradients(jax.random.fold_in(keys[8], 71), 0)
    weights = gaussian(keys[1], (NB, MODEL_WIDTH, MODEL_WIDTH), MODEL_WIDTH ** -0.5, 0.1875, ((1, 8), (2, 4)), jnp.float32)
    owner_list = draw_owner_list(jax.random.fold_in(keys[8], 71), 0)
    left_gram_stats = gaussian(keys[3], (SLOT_TOTAL, MODEL_WIDTH, MODEL_WIDTH), 1.0, 6.0, ((0, 8), (1, 4)), jnp.float32)
    right_gram_stats = gaussian(keys[4], (SLOT_TOTAL, MODEL_WIDTH, MODEL_WIDTH), 1.0, 6.0, ((0, 8), (1, 4)), jnp.float32)
    left_root = draw_left_root(jax.random.fold_in(keys[8], 71), 0)
    right_root = draw_right_root(jax.random.fold_in(keys[8], 71), 0)
    adam_second_moment = jnp.clip(jnp.exp(math.log(10.0) - 4.6051702 * jax.random.uniform(keys[7], (SLOT_TOTAL, MODEL_WIDTH, MODEL_WIDTH), jnp.float32) ** block_scale(keys[7], (SLOT_TOTAL, MODEL_WIDTH, MODEL_WIDTH), ((0, 8), (2, 4)), -0.2, 0.2)), 0.1, 10.0)
    return dict(gradients=gradients, weights=weights, owner_list=owner_list, left_gram_stats=left_gram_stats, right_gram_stats=right_gram_stats, left_root=left_root, right_root=right_root, adam_second_moment=adam_second_moment)


stat_decay = 0.95
moment_decay = 0.95
learn_rate = 0.02
graft_eps = 1e-06

def slot_table(owner_list):
    count = owner_list.shape[0]
    positions = jnp.arange(count, dtype=jnp.int32)
    earlier = (owner_list[:, None] == owner_list[None, :]) & (positions[None, :] < positions[:, None])
    slot_rank = lax.optimization_barrier(jnp.sum(earlier.astype(jnp.int32), axis=1)).astype(jnp.int32)
    return (slot_rank, (owner_list * SLOTS + slot_rank).astype(jnp.int32))

def reference(gradients, weights, owner_list, left_gram_stats, right_gram_stats, left_root, right_root, adam_second_moment):
    slot_rank, slot_index = slot_table(owner_list)

    def one_block(item):
        block, place = item
        grad_full = block.astype(jnp.float32)
        gram_left = jnp.dot(block, block.T, preferred_element_type=jnp.float32) / MODEL_WIDTH
        gram_right = jnp.dot(block.T, block, preferred_element_type=jnp.float32) / MODEL_WIDTH
        left_new = stat_decay * left_gram_stats[place] + gram_left
        right_new = stat_decay * right_gram_stats[place] + gram_right
        moment_new = moment_decay * adam_second_moment[place] + (1.0 - moment_decay) * grad_full * grad_full
        adam_dir = grad_full / jnp.sqrt(moment_new)
        product = jnp.dot(block, right_root[place], preferred_element_type=jnp.float32).astype(jnp.bfloat16)
        precond = jnp.dot(left_root[place], product, preferred_element_type=jnp.float32)
        ratio = jnp.sqrt(jnp.mean(adam_dir * adam_dir)) / jnp.sqrt(jnp.mean(precond * precond) + graft_eps)
        return (left_new, right_new, moment_new, -learn_rate * ratio * precond)
    left_live, right_live, moment_live, updates = lax.map(one_block, (gradients, slot_index))
    new_left = (stat_decay * left_gram_stats).at[slot_index].set(left_live)
    new_right = (stat_decay * right_gram_stats).at[slot_index].set(right_live)
    new_moment = (moment_decay * adam_second_moment).at[slot_index].set(moment_live)
    new_weights = weights + updates
    return (new_weights, new_left, new_right, new_moment)
```

```python
import functools

import jax
import jax.numpy as jnp
from jax import lax
from jax.experimental import pallas as pl
from jax.experimental.pallas import tpu as pltpu
from jax.sharding import PartitionSpec as P

MODEL_WIDTH = 1152
SLOTS = 2


stat_decay = 0.95
moment_decay = 0.95
learn_rate = 0.02
graft_eps = 1e-06


def slot_table(owner_list):
    count = owner_list.shape[0]
    positions = jnp.arange(count, dtype=jnp.int32)
    earlier = (owner_list[:, None] == owner_list[None, :]) & (
        positions[None, :] < positions[:, None]
    )
    slot_rank = jnp.sum(earlier.astype(jnp.int32), axis=1)
    return (slot_rank, owner_list * SLOTS + slot_rank)


def body(
    gradients,
    weights,
    owner_list,
    left_gram_stats,
    right_gram_stats,
    left_root,
    right_root,
    adam_second_moment,
):
    shard_count = lax.axis_size("shard")
    tensor_count = lax.axis_size("tensor")
    slots = left_gram_stats.shape[0]
    row_count = gradients.shape[1]
    part_width = gradients.shape[2]
    block_count = owner_list.shape[0]
    slot_rank, slot_index = slot_table(owner_list)
    all_slots = jnp.arange(shard_count * slots, dtype=jnp.int32)
    block_ids = jnp.arange(block_count, dtype=jnp.int32)
    matches = slot_index[None, :] == all_slots[:, None]
    occupied = jnp.any(matches, axis=1)
    source_block = jnp.sum(jnp.where(matches, block_ids[None, :], 0), axis=1)
    outgoing = jnp.where(
        occupied[:, None, None],
        jnp.take(gradients, source_block, axis=0),
        jnp.zeros((), jnp.bfloat16),
    )
    layered = outgoing.reshape(shard_count, 1, slots, row_count, part_width)
    layered = jnp.broadcast_to(layered, (shard_count, tensor_count, slots, row_count, part_width))
    layered = layered.reshape(shard_count * tensor_count * slots, row_count, part_width)
    arrived = lax.all_to_all(layered, ("shard", "tensor"), split_axis=0, concat_axis=0, tiled=True)
    arrived = arrived.reshape(shard_count, tensor_count, slots, row_count, part_width)
    full_grad = jnp.transpose(arrived, (2, 0, 3, 1, 4)).reshape(
        slots, shard_count * row_count, tensor_count * part_width
    )
    tensor_pos = lax.axis_index("tensor")
    own_start = tensor_pos * part_width
    grad_rows = lax.dynamic_slice_in_dim(full_grad, own_start, part_width, 1)
    grad_cols = lax.dynamic_slice_in_dim(full_grad, own_start, part_width, 2)
    gram_left = (
        jnp.einsum("sij,skj->sik", grad_rows, full_grad, preferred_element_type=jnp.float32)
        / MODEL_WIDTH
    )
    gram_right = (
        jnp.einsum("sji,sjk->sik", grad_cols, full_grad, preferred_element_type=jnp.float32)
        / MODEL_WIDTH
    )
    new_left = stat_decay * left_gram_stats + gram_left
    new_right = stat_decay * right_gram_stats + gram_right
    grad_part = grad_cols.astype(jnp.float32)
    new_moment = moment_decay * adam_second_moment + (1.0 - moment_decay) * grad_part * grad_part
    adam_dir = grad_part / jnp.sqrt(new_moment)
    product = jnp.einsum(
        "sij,sjk->sik", full_grad, right_root, preferred_element_type=jnp.float32
    ).astype(jnp.bfloat16)
    precond = jnp.einsum(
        "sij,sjk->sik",
        lax.all_gather(left_root, "tensor", axis=2, tiled=True),
        product,
        preferred_element_type=jnp.float32,
    )
    adam_sum = jnp.sum(adam_dir * adam_dir, axis=(1, 2))
    precond_sum = jnp.sum(precond * precond, axis=(1, 2))
    adam_total, precond_total = lax.psum((adam_sum, precond_sum), "tensor")
    entries = float(MODEL_WIDTH * MODEL_WIDTH)
    ratio = jnp.sqrt(adam_total / entries) / jnp.sqrt(precond_total / entries + graft_eps)
    update = (-learn_rate * ratio)[:, None, None] * precond
    update = update.reshape(slots, shard_count, row_count, part_width)
    returned = lax.all_to_all(update, "shard", split_axis=1, concat_axis=1, tiled=True)
    returned = jnp.transpose(returned, (1, 0, 2, 3)).reshape(
        shard_count * slots, row_count, part_width
    )
    block_update = jnp.take(returned, slot_index, axis=0)
    new_weights = weights + block_update
    return (new_weights, new_left, new_right, new_moment)


MESH = pl.DeviceIdType.MESH
TILE = 384
NT = (((1,), (1,)), ((), ()))
NN = (((1,), (0,)), ((), ()))


def mm(a, b, dims):
    return lax.dot_general(a, b, dims, preferred_element_type=jnp.float32)


def step_kernel(
    shards,
    owner_ref,
    grad_ref,
    right_root_ref,
    left_root_hbm,
    left_hbm,
    right_hbm,
    moment_hbm,
    update_ref,
    new_left_hbm,
    new_right_hbm,
    new_moment_hbm,
    out_buf,
    own,
    grad_t,
    left_root,
    prod_t,
    back_out,
    back_in,
    left,
    right,
    moment,
    sums,
    ratios,
    s1_send,
    s1_recv,
    g_send,
    g_recv,
    l_send,
    l_recv,
    b_send,
    b_recv,
    sum_send,
    sum_recv,
    rat_send,
    rat_recv,
    in_sem,
    out_sem,
):
    me = lax.axis_index("shard")
    t = lax.axis_index("tensor")
    sib = t + 1 - 2 * lax.rem(t, 2)
    across = lax.rem(t + 2, 4)
    diag = lax.rem(sib + 2, 4)
    blocks, rows, width = grad_ref.shape
    side = rows * shards
    slots = left.shape[0]
    t_rows = pl.ds(pl.multiple_of(t * width, 32), width)
    across_rows = pl.ds(pl.multiple_of(across * width, 32), width)

    def peer(d):
        return lax.rem(me + d, shards)

    def strip(s):
        return pl.ds(pl.multiple_of(s * rows, 16), rows)

    root_in = [
        pltpu.make_async_copy(
            left_root_hbm.at[k], left_root.at[k, t_rows, :], in_sem.at[k]
        )
        for k in range(slots)
    ]
    stat_in = [
        pltpu.make_async_copy(src, dst, in_sem.at[slots + i])
        for i, (src, dst) in enumerate(
            ((moment_hbm, moment), (left_hbm, left), (right_hbm, right))
        )
    ]
    for copy in root_in:
        copy.start()

    barrier = pltpu.get_barrier_semaphore()

    @pl.loop(1, shards)
    def _(d):
        pl.semaphore_signal(barrier, inc=1, device_id=(peer(d), t), device_id_type=MESH)

    for other in (sib, across, diag):
        pl.semaphore_signal(barrier, inc=1, device_id=(me, other), device_id_type=MESH)

    owners = [owner_ref[b] for b in range(blocks)]
    slot_of = []
    for b in range(blocks):
        place = owners[b] * slots
        for c in range(b):
            place = place + jnp.where(owners[c] == owners[b], 1, 0)
        slot_of.append(place)

    def pick(k, s):
        source = jnp.int32(0)
        found = jnp.int32(0)
        for b in range(blocks):
            hit = slot_of[b] == s * slots + k
            source = jnp.where(hit, b, source)
            found = jnp.where(hit, 1, found)
        block = grad_ref[source]
        return jnp.where(found > 0, block, jnp.zeros_like(block))

    pl.semaphore_wait(barrier, shards - 1 + 3)

    def s1_copy(k, d):
        s = peer(d)
        return pltpu.make_async_remote_copy(
            src_ref=out_buf.at[k, s],
            dst_ref=own.at[k, strip(me), :],
            send_sem=s1_send.at[k, s],
            recv_sem=s1_recv.at[k, me],
            device_id=(s, t),
            device_id_type=MESH,
        )

    def s1_arrival(k, d):
        s = peer(d)
        return pltpu.make_async_remote_copy(
            src_ref=out_buf.at[k, s],
            dst_ref=own.at[k, strip(s), :],
            send_sem=s1_send.at[k, s],
            recv_sem=s1_recv.at[k, s],
            device_id=(s, t),
            device_id_type=MESH,
        )

    def panel_copy(buf, send, recv, k, panel, hop, target):
        return pltpu.make_async_remote_copy(
            src_ref=buf.at[k, panel, :],
            dst_ref=buf.at[k, panel, :],
            send_sem=send.at[k, hop],
            recv_sem=recv.at[k, hop],
            device_id=(me, target),
            device_id_type=MESH,
        )

    def root_copies(k):
        return (
            panel_copy(left_root, l_send, l_recv, k, t_rows, 0, sib),
            panel_copy(left_root, l_send, l_recv, k, t_rows, 1, across),
            panel_copy(left_root, l_send, l_recv, k, across_rows, 2, sib),
        )

    def grad_copies(k):
        return (
            panel_copy(grad_t, g_send, g_recv, k, t_rows, 0, sib),
            panel_copy(grad_t, g_send, g_recv, k, t_rows, 1, across),
            panel_copy(grad_t, g_send, g_recv, k, across_rows, 2, sib),
        )

    def send_strips(k):
        @pl.loop(1, shards)
        def _(d):
            s = peer(d)
            out_buf[k, s] = pick(k, s)
            s1_copy(k, d).start()

        own[k, strip(me), :] = pick(k, me)

    root_moves = [root_copies(k) for k in range(slots)]
    grad_moves = [grad_copies(k) for k in range(slots)]

    send_strips(0)
    for k in range(slots):
        root_in[k].wait()
        root_moves[k][1].start()
        root_moves[k][0].start()
        if k + 1 < slots:
            send_strips(k + 1)
    for copy in stat_in:
        copy.start()

    at_row = lax.broadcasted_iota(jnp.int32, (width, width), 0)
    at_col = lax.broadcasted_iota(jnp.int32, (width, width), 1)
    unit = (at_row == at_col).astype(jnp.bfloat16)

    def turn_panel(k):
        @pl.loop(1, shards)
        def _(d):
            s1_arrival(k, d).wait_recv()

        for j in range(side // TILE):
            piece = own[k, j * TILE : (j + 1) * TILE, :]
            grad_t[k, t_rows, j * TILE : (j + 1) * TILE] = mm(unit, piece, NT).astype(
                jnp.bfloat16
            )
        grad_moves[k][1].start()
        grad_moves[k][0].start()

    def pass_on(moves):
        moves[1].wait_recv()
        moves[2].start()

    chunk = 96

    def moments(k):
        def one(j, total):
            at = pl.ds(pl.multiple_of(j * chunk, 32), chunk)
            g = grad_t[k, pl.ds(pl.multiple_of(t * width + j * chunk, 32), chunk), :].astype(
                jnp.float32
            )
            fresh = moment_decay * moment[k, at, :] + (1.0 - moment_decay) * g * g
            moment[k, at, :] = fresh
            direction = g / jnp.sqrt(fresh)
            return total + jnp.sum(direction * direction, axis=0, keepdims=True)

        total = lax.fori_loop(0, width // chunk, one, jnp.zeros((1, side), jnp.float32))
        sums[t, 0, k] = jnp.full((8, 128), jnp.sum(total), jnp.float32)

    def back_copy(k, d):
        s = peer(d)
        return pltpu.make_async_remote_copy(
            src_ref=back_out.at[k, s],
            dst_ref=back_in.at[me * slots + k],
            send_sem=b_send.at[k, s],
            recv_sem=b_recv.at[k, me],
            device_id=(s, t),
            device_id_type=MESH,
        )

    def back_arrival(k, d):
        s = peer(d)
        return pltpu.make_async_remote_copy(
            src_ref=back_out.at[k, s],
            dst_ref=back_in.at[s * slots + k],
            send_sem=b_send.at[k, s],
            recv_sem=b_recv.at[k, s],
            device_id=(s, t),
            device_id_type=MESH,
        )

    def precondition(k):
        @pl.loop(0, side // TILE)
        def _(j):
            at = pl.ds(pl.multiple_of(j * TILE, 128), TILE)
            prod_t[k, :, at] = mm(right_root_ref[k], grad_t[k, :, at], NN).astype(jnp.bfloat16)

        for hop in (0, 2):
            root_moves[k][hop].wait_recv()

        def piece(s):
            return mm(left_root[k, strip(s), :], prod_t[k], NT)

        def one(d, total):
            s = peer(d)
            part = piece(s)
            back_out[k, s] = part.astype(jnp.bfloat16)
            back_copy(k, d).start()
            return total + jnp.sum(part * part, axis=0, keepdims=True)

        total = lax.fori_loop(1, shards, one, jnp.zeros((1, width), jnp.float32))
        part = piece(me)
        back_in[me * slots + k] = part.astype(jnp.bfloat16)
        total = total + jnp.sum(part * part, axis=0, keepdims=True)
        sums[t, 1, k] = jnp.full((8, 128), jnp.sum(total), jnp.float32)

    start = pl.multiple_of(t * width // 128 * 128, 128)
    shift = t * width - start
    sel_row = lax.broadcasted_iota(jnp.int32, (width, TILE), 0)
    sel_col = lax.broadcasted_iota(jnp.int32, (width, TILE), 1)
    select = (sel_col == sel_row + shift).astype(jnp.bfloat16)

    def grams(k):
        rows_t = mm(select, grad_t[k, :, pl.ds(start, TILE)], NT).astype(jnp.bfloat16)
        out = []

        @pl.loop(0, side // TILE)
        def _(j):
            at = pl.ds(pl.multiple_of(j * TILE, 128), TILE)
            left[k, :, at] = stat_decay * left[k, :, at] + mm(
                rows_t, grad_t[k, :, at], NN
            ) / MODEL_WIDTH
            right[k, :, at] = stat_decay * right[k, :, at] + mm(
                grad_t[k, t_rows, :], grad_t[k, at, :], NT
            ) / MODEL_WIDTH

        for i, (src, dst) in enumerate(
            ((left, new_left_hbm), (right, new_right_hbm), (moment, new_moment_hbm))
        ):
            copy = pltpu.make_async_copy(src.at[k], dst.at[k], out_sem.at[k, i])
            copy.start()
            out.append(copy)
        return out

    for k in range(slots):
        turn_panel(k)
        pass_on(root_moves[k])
    for copy in stat_in:
        copy.wait()
    for k in range(slots):
        moments(k)

    outs = []
    for k in range(slots):
        pass_on(grad_moves[k])
        for hop in (0, 2):
            grad_moves[k][hop].wait_recv()
        precondition(k)
        if k + 1 < slots:
            outs += grams(k)

    sum_moves = [
        pltpu.make_async_remote_copy(
            src_ref=sums.at[t],
            dst_ref=sums.at[t],
            send_sem=sum_send.at[i],
            recv_sem=sum_recv.at[i],
            device_id=(me, other),
            device_id_type=MESH,
        )
        for i, other in enumerate((sib, across, diag))
    ]
    for move in sum_moves:
        move.start()
    outs += grams(slots - 1)
    for move in sum_moves:
        move.wait_recv()

    entries = float(MODEL_WIDTH * MODEL_WIDTH)
    totals = sums[0] + sums[1] + sums[2] + sums[3]
    ratio = jnp.sqrt(totals[0] / entries) / jnp.sqrt(totals[1] / entries + graft_eps)
    mine = pl.ds(me * slots, slots)
    ratios[mine] = ratio

    def ratio_copy(d):
        s = peer(d)
        return pltpu.make_async_remote_copy(
            src_ref=ratios.at[mine],
            dst_ref=ratios.at[mine],
            send_sem=rat_send.at[s],
            recv_sem=rat_recv.at[me],
            device_id=(s, t),
            device_id_type=MESH,
        )

    def ratio_arrival(d):
        s = peer(d)
        theirs = pl.ds(s * slots, slots)
        return pltpu.make_async_remote_copy(
            src_ref=ratios.at[theirs],
            dst_ref=ratios.at[theirs],
            send_sem=rat_send.at[s],
            recv_sem=rat_recv.at[s],
            device_id=(s, t),
            device_id_type=MESH,
        )

    @pl.loop(1, shards)
    def _(d):
        ratio_copy(d).start()

    @pl.loop(1, shards)
    def _(d):
        ratio_arrival(d).wait_recv()
        for k in range(slots):
            back_arrival(k, d).wait_recv()

    for b in range(blocks):
        scale = -learn_rate * ratios[slot_of[b]][0:1, 0:1]
        update_ref[b] = scale * back_in[slot_of[b]].astype(jnp.float32)

    @pl.loop(1, shards)
    def _(d):
        ratio_copy(d).wait_send()
        for k in range(slots):
            s1_copy(k, d).wait_send()
            back_copy(k, d).wait_send()

    for k in range(slots):
        for move in root_moves[k] + grad_moves[k]:
            move.wait_send()
    for move in sum_moves:
        move.wait_send()
    for copy in outs:
        copy.wait()


def kernel_body(
    gradients,
    weights,
    owner_list,
    left_gram_stats,
    right_gram_stats,
    left_root,
    right_root,
    adam_second_moment,
):
    shards = lax.axis_size("shard")
    blocks, rows, width = gradients.shape
    slots = left_gram_stats.shape[0]
    side = rows * shards
    bf16, f32 = jnp.bfloat16, jnp.float32
    flip = lambda a: jnp.transpose(a, (0, 2, 1))
    hbm = pl.BlockSpec(memory_space=pl.ANY)
    vmem = pl.BlockSpec(memory_space=pltpu.VMEM)
    dma = lambda *shape: pltpu.SemaphoreType.DMA(shape)
    stat = jax.ShapeDtypeStruct((slots, width, side), f32)
    update, new_left, new_right, new_moment = pl.pallas_call(
        functools.partial(step_kernel, shards),
        out_shape=(jax.ShapeDtypeStruct((blocks, rows, width), f32), stat, stat, stat),
        in_specs=[pl.BlockSpec(memory_space=pltpu.SMEM), vmem, vmem, hbm, hbm, hbm, hbm],
        out_specs=(vmem, hbm, hbm, hbm),
        scratch_shapes=[
            pltpu.VMEM((slots, shards, rows, width), bf16),
            pltpu.VMEM((slots, side, width), bf16),
            pltpu.VMEM((slots, side, side), bf16),
            pltpu.VMEM((slots, side, side), bf16),
            pltpu.VMEM((slots, width, side), bf16),
            pltpu.VMEM((slots, shards, rows, width), bf16),
            pltpu.VMEM((slots * shards, rows, width), bf16),
            pltpu.VMEM((slots, width, side), f32),
            pltpu.VMEM((slots, width, side), f32),
            pltpu.VMEM((slots, width, side), f32),
            pltpu.VMEM((4, 2, slots, 8, 128), f32),
            pltpu.VMEM((slots * shards, 8, 128), f32),
            dma(slots, shards),
            dma(slots, shards),
            dma(slots, 3),
            dma(slots, 3),
            dma(slots, 3),
            dma(slots, 3),
            dma(slots, shards),
            dma(slots, shards),
            dma(3),
            dma(3),
            dma(shards),
            dma(shards),
            dma(slots + 3),
            dma(slots, 3),
        ],
        compiler_params=pltpu.CompilerParams(
            collective_id=0, has_side_effects=True, vmem_limit_bytes=52 * 2**20
        ),
    )(
        owner_list,
        gradients,
        flip(right_root),
        flip(left_root),
        left_gram_stats,
        right_gram_stats,
        flip(adam_second_moment),
    )
    return (weights + update, new_left, new_right, flip(new_moment))


def fits(mesh, gradients):
    shards, tensor = mesh.shape["shard"], mesh.shape["tensor"]
    rows, width = gradients.shape[1] // shards, gradients.shape[2] // tensor
    return (
        tensor == 4
        and rows % 16 == 0
        and width % 96 == 0
        and width <= TILE - 96
        and gradients.shape[1] % TILE == 0
    )


def solution(mesh):
    def run(gradients, *others):
        chosen = kernel_body if fits(mesh, gradients) else body
        return mapped(chosen)(gradients, *others)

    mapped = lambda chosen: jax.shard_map(
        chosen,
        mesh=mesh,
        in_specs=(
            P(None, "shard", "tensor"),
            P(None, "shard", "tensor"),
            P(),
            P("shard", "tensor", None),
            P("shard", "tensor", None),
            P("shard", None, "tensor"),
            P("shard", None, "tensor"),
            P("shard", None, "tensor"),
        ),
        out_specs=(
            P(None, "shard", "tensor"),
            P("shard", "tensor", None),
            P("shard", "tensor", None),
            P("shard", None, "tensor"),
        ),
        check_vma=False,
    )
    return run
```

```python
import functools

import jax
import jax.numpy as jnp
from jax import lax
from jax.experimental import pallas as pl
from jax.experimental.pallas import tpu as pltpu
from jax.sharding import PartitionSpec as P

MODEL_WIDTH = 1152
SLOTS = 2


stat_decay = 0.95
moment_decay = 0.95
learn_rate = 0.02
graft_eps = 1e-06


def slot_table(owner_list):
    count = owner_list.shape[0]
    positions = jnp.arange(count, dtype=jnp.int32)
    earlier = (owner_list[:, None] == owner_list[None, :]) & (
        positions[None, :] < positions[:, None]
    )
    slot_rank = jnp.sum(earlier.astype(jnp.int32), axis=1)
    return (slot_rank, owner_list * SLOTS + slot_rank)


def body(
    gradients,
    weights,
    owner_list,
    left_gram_stats,
    right_gram_stats,
    left_root,
    right_root,
    adam_second_moment,
):
    shard_count = lax.axis_size("shard")
    tensor_count = lax.axis_size("tensor")
    slots = left_gram_stats.shape[0]
    row_count = gradients.shape[1]
    part_width = gradients.shape[2]
    block_count = owner_list.shape[0]
    slot_rank, slot_index = slot_table(owner_list)
    all_slots = jnp.arange(shard_count * slots, dtype=jnp.int32)
    block_ids = jnp.arange(block_count, dtype=jnp.int32)
    matches = slot_index[None, :] == all_slots[:, None]
    occupied = jnp.any(matches, axis=1)
    source_block = jnp.sum(jnp.where(matches, block_ids[None, :], 0), axis=1)
    outgoing = jnp.where(
        occupied[:, None, None],
        jnp.take(gradients, source_block, axis=0),
        jnp.zeros((), jnp.bfloat16),
    )
    layered = outgoing.reshape(shard_count, 1, slots, row_count, part_width)
    layered = jnp.broadcast_to(layered, (shard_count, tensor_count, slots, row_count, part_width))
    layered = layered.reshape(shard_count * tensor_count * slots, row_count, part_width)
    arrived = lax.all_to_all(layered, ("shard", "tensor"), split_axis=0, concat_axis=0, tiled=True)
    arrived = arrived.reshape(shard_count, tensor_count, slots, row_count, part_width)
    full_grad = jnp.transpose(arrived, (2, 0, 3, 1, 4)).reshape(
        slots, shard_count * row_count, tensor_count * part_width
    )
    tensor_pos = lax.axis_index("tensor")
    own_start = tensor_pos * part_width
    grad_rows = lax.dynamic_slice_in_dim(full_grad, own_start, part_width, 1)
    grad_cols = lax.dynamic_slice_in_dim(full_grad, own_start, part_width, 2)
    gram_left = (
        jnp.einsum("sij,skj->sik", grad_rows, full_grad, preferred_element_type=jnp.float32)
        / MODEL_WIDTH
    )
    gram_right = (
        jnp.einsum("sji,sjk->sik", grad_cols, full_grad, preferred_element_type=jnp.float32)
        / MODEL_WIDTH
    )
    new_left = stat_decay * left_gram_stats + gram_left
    new_right = stat_decay * right_gram_stats + gram_right
    grad_part = grad_cols.astype(jnp.float32)
    new_moment = moment_decay * adam_second_moment + (1.0 - moment_decay) * grad_part * grad_part
    adam_dir = grad_part / jnp.sqrt(new_moment)
    product = jnp.einsum(
        "sij,sjk->sik", full_grad, right_root, preferred_element_type=jnp.float32
    ).astype(jnp.bfloat16)
    precond = jnp.einsum(
        "sij,sjk->sik",
        lax.all_gather(left_root, "tensor", axis=2, tiled=True),
        product,
        preferred_element_type=jnp.float32,
    )
    adam_sum = jnp.sum(adam_dir * adam_dir, axis=(1, 2))
    precond_sum = jnp.sum(precond * precond, axis=(1, 2))
    adam_total, precond_total = lax.psum((adam_sum, precond_sum), "tensor")
    entries = float(MODEL_WIDTH * MODEL_WIDTH)
    ratio = jnp.sqrt(adam_total / entries) / jnp.sqrt(precond_total / entries + graft_eps)
    update = (-learn_rate * ratio)[:, None, None] * precond
    update = update.reshape(slots, shard_count, row_count, part_width)
    returned = lax.all_to_all(update, "shard", split_axis=1, concat_axis=1, tiled=True)
    returned = jnp.transpose(returned, (1, 0, 2, 3)).reshape(
        shard_count * slots, row_count, part_width
    )
    block_update = jnp.take(returned, slot_index, axis=0)
    new_weights = weights + block_update
    return (new_weights, new_left, new_right, new_moment)


MESH = pl.DeviceIdType.MESH
TILE = 384
NT = (((1,), (1,)), ((), ()))
NN = (((1,), (0,)), ((), ()))


def mm(a, b, dims):
    return lax.dot_general(a, b, dims, preferred_element_type=jnp.float32)


def step_kernel(
    shards,
    owner_ref,
    grad_ref,
    right_root_ref,
    left_root_hbm,
    left_hbm,
    right_hbm,
    moment_hbm,
    update_ref,
    new_left_hbm,
    new_right_hbm,
    new_moment_hbm,
    out_0,
    out_1,
    own_0,
    own_1,
    grad_t,
    left_root,
    prod_t,
    tail_t,
    back_0,
    back_1,
    in_0,
    in_1,
    left,
    right,
    moment,
    sums,
    ratios,
    s1_send,
    s1_recv,
    g_send,
    g_recv,
    l_send,
    l_recv,
    b_send,
    b_recv,
    sum_send,
    sum_recv,
    rat_send,
    rat_recv,
    in_sem,
    out_sem,
):
    me = lax.axis_index("shard")
    t = lax.axis_index("tensor")
    sib = t + 1 - 2 * lax.rem(t, 2)
    across = lax.rem(t + 2, 4)
    diag = lax.rem(sib + 2, 4)
    blocks, rows, width = grad_ref.shape
    side = rows * shards
    slots = left.shape[0]
    main = width // 128 * 128
    tail = width - main
    wide = main + 128
    half = 2 * width
    low, high = half // 128 * 128, -(-half // 128) * 128
    y = t // 2
    out_bufs, owns = (out_0, out_1), (own_0, own_1)
    backs, ins = (back_0, back_1), (in_0, in_1)
    t_rows = pl.ds(pl.multiple_of(t * width, 32), width)
    across_rows = pl.ds(pl.multiple_of(across * width, 32), width)

    def peer(d):
        return lax.rem(me + d, shards)

    def strip(s):
        return pl.ds(pl.multiple_of(s * rows, 16), rows)

    root_in = [
        pltpu.make_async_copy(
            left_root_hbm.at[k], left_root.at[k, t_rows, :], in_sem.at[k]
        )
        for k in range(slots)
    ]
    stat_in = [
        pltpu.make_async_copy(src, dst, in_sem.at[slots + i])
        for i, (src, dst) in enumerate(
            ((moment_hbm, moment), (left_hbm, left), (right_hbm, right))
        )
    ]
    for copy in root_in:
        copy.start()

    barrier = pltpu.get_barrier_semaphore()

    @pl.loop(1, shards)
    def _(d):
        pl.semaphore_signal(barrier, inc=1, device_id=(peer(d), t), device_id_type=MESH)

    for other in (sib, across, diag):
        pl.semaphore_signal(barrier, inc=1, device_id=(me, other), device_id_type=MESH)

    owners = [owner_ref[b] for b in range(blocks)]
    slot_of = []
    for b in range(blocks):
        place = owners[b] * slots
        for c in range(b):
            place = place + jnp.where(owners[c] == owners[b], 1, 0)
        slot_of.append(place)

    def pick(k, s):
        source = jnp.int32(0)
        found = jnp.int32(0)
        for b in range(blocks):
            hit = slot_of[b] == s * slots + k
            source = jnp.where(hit, b, source)
            found = jnp.where(hit, 1, found)
        block = grad_ref[source]
        return jnp.where(found > 0, block, jnp.zeros_like(block))

    def shifted(count, lanes, shift):
        row = lax.broadcasted_iota(jnp.int32, (count, lanes), 0)
        col = lax.broadcasted_iota(jnp.int32, (count, lanes), 1)
        return (col == row + shift).astype(jnp.bfloat16)

    def pack(s):
        first, second = pick(0, s), pick(1, s)
        ends = mm(first[:, main:], shifted(tail, 128, 0), NN) + mm(
            second[:, main:], shifted(tail, 128, tail), NN
        )
        return first[:, :main], ends.astype(jnp.bfloat16), second[:, :main]

    pl.semaphore_wait(barrier, shards - 1 + 3)

    def s1_copy(k, d):
        s = peer(d)
        return pltpu.make_async_remote_copy(
            src_ref=out_bufs[k].at[s],
            dst_ref=owns[k].at[strip(me), :],
            send_sem=s1_send.at[k, s],
            recv_sem=s1_recv.at[k, me],
            device_id=(s, t),
            device_id_type=MESH,
        )

    def s1_arrival(k, d):
        s = peer(d)
        return pltpu.make_async_remote_copy(
            src_ref=out_bufs[k].at[s],
            dst_ref=owns[k].at[strip(s), :],
            send_sem=s1_send.at[k, s],
            recv_sem=s1_recv.at[k, s],
            device_id=(s, t),
            device_id_type=MESH,
        )

    def panel_copy(buf, send, recv, k, panel, hop, target, lanes=slice(None)):
        return pltpu.make_async_remote_copy(
            src_ref=buf.at[k, panel, lanes],
            dst_ref=buf.at[k, panel, lanes],
            send_sem=send.at[k, hop],
            recv_sem=recv.at[k, hop],
            device_id=(me, target),
            device_id_type=MESH,
        )

    def window(which):
        return pl.ds(pl.multiple_of(low * which, 128), high)

    def mirror(k):
        root_moves[k][0].wait_recv()
        turn = shifted(half, high, (half - low) * (1 - y))

        @pl.loop(0, low // 256)
        def _(j):
            here = pl.ds(pl.multiple_of(high * y + 256 * j, 128), 256)
            there = pl.ds(pl.multiple_of(half * (1 - y), 32), half)
            piece = left_root[k, here, window(1 - y)]
            left_root[k, there, here] = mm(turn, piece, NT).astype(jnp.bfloat16)

    def root_copies(k):
        return (
            panel_copy(left_root, l_send, l_recv, k, t_rows, 0, sib),
            panel_copy(left_root, l_send, l_recv, k, t_rows, 1, across, window(y)),
            panel_copy(left_root, l_send, l_recv, k, across_rows, 2, sib, window(1 - y)),
        )

    def grad_copies(k):
        return (
            panel_copy(grad_t, g_send, g_recv, k, t_rows, 0, sib),
            panel_copy(grad_t, g_send, g_recv, k, t_rows, 1, across),
            panel_copy(grad_t, g_send, g_recv, k, across_rows, 2, sib),
        )

    root_moves = [root_copies(k) for k in range(slots)]
    grad_moves = [grad_copies(k) for k in range(slots)]

    @pl.loop(1, shards)
    def _(d):
        s = peer(d)
        first, ends, second = pack(s)
        out_0[s, :, 0:main] = first
        out_0[s, :, main:wide] = ends
        out_1[s] = second
        s1_copy(0, d).start()

    for k in range(slots):
        root_in[k].wait()
        root_moves[k][1].start()
        root_moves[k][0].start()

    @pl.loop(1, shards)
    def _(d):
        s1_copy(1, d).start()

    first, ends, second = pack(me)
    own_0[strip(me), 0:main] = first
    own_0[strip(me), main:wide] = ends
    own_1[strip(me), :] = second
    prod_t[1, width:, :] = jnp.zeros((wide - width, side), jnp.bfloat16)
    tail_t[...] = jnp.zeros((128, side), jnp.bfloat16)
    for copy in stat_in:
        copy.start()

    def turn_panel(k):
        @pl.loop(1, shards)
        def _(d):
            s1_arrival(k, d).wait_recv()

        for j in range(side // TILE):
            at = slice(j * TILE, (j + 1) * TILE)
            if k == 0:
                grad_t[0, t_rows, at] = mm(shifted(width, wide, 0), own_0[at, :], NT).astype(
                    jnp.bfloat16
                )
            else:
                top = pl.ds(pl.multiple_of(t * width, 32), main)
                end = pl.ds(pl.multiple_of(t * width + main, 32), tail)
                grad_t[1, top, at] = mm(shifted(main, main, 0), own_1[at, :], NT).astype(
                    jnp.bfloat16
                )
                grad_t[1, end, at] = mm(
                    shifted(tail, 128, tail), own_0[at, main:wide], NT
                ).astype(jnp.bfloat16)
        grad_moves[k][1].start()
        grad_moves[k][0].start()

    def pass_on(moves):
        moves[1].wait_recv()
        moves[2].start()

    chunk = 96

    def moments(k):
        def one(j, total):
            at = pl.ds(pl.multiple_of(j * chunk, 32), chunk)
            g = grad_t[k, pl.ds(pl.multiple_of(t * width + j * chunk, 32), chunk), :].astype(
                jnp.float32
            )
            fresh = moment_decay * moment[k, at, :] + (1.0 - moment_decay) * g * g
            moment[k, at, :] = fresh
            direction = g / jnp.sqrt(fresh)
            return total + jnp.sum(direction * direction, axis=0, keepdims=True)

        total = lax.fori_loop(0, width // chunk, one, jnp.zeros((1, side), jnp.float32))
        sums[t, 0, k] = jnp.full((8, 128), jnp.sum(total), jnp.float32)

    def back_copy(k, d):
        s = peer(d)
        return pltpu.make_async_remote_copy(
            src_ref=backs[k].at[s],
            dst_ref=ins[k].at[me],
            send_sem=b_send.at[k, s],
            recv_sem=b_recv.at[k, me],
            device_id=(s, t),
            device_id_type=MESH,
        )

    def back_arrival(k, d):
        s = peer(d)
        return pltpu.make_async_remote_copy(
            src_ref=backs[k].at[s],
            dst_ref=ins[k].at[s],
            send_sem=b_send.at[k, s],
            recv_sem=b_recv.at[k, s],
            device_id=(s, t),
            device_id_type=MESH,
        )

    def precondition(k):
        @pl.loop(0, side // TILE)
        def _(j):
            at = pl.ds(pl.multiple_of(j * TILE, 128), TILE)
            prod_t[k, 0:width, at] = mm(right_root_ref[k], grad_t[k, :, at], NN).astype(
                jnp.bfloat16
            )

        if k == 0:
            tail_t[tail : 2 * tail, :] = prod_t[0, main:width, :]
        root_moves[k][2].wait_recv()

        def squares(part):
            return jnp.sum(part * part, axis=0, keepdims=True)

        def pieces(s, put, total):
            if k == 0:
                part = mm(left_root[0, strip(s), :], prod_t[0, 0:main, :], NT)
                put(part)
                return total[0] + squares(part), total[1]
            part = mm(left_root[1, strip(s), :], prod_t[1], NT)
            ends = mm(left_root[0, strip(s), :], tail_t[...], NT)
            put(part, ends)
            return total[0] + squares(part), total[1] + squares(ends)

        def put_in(ref, s):
            def put(part, ends=None):
                if ends is None:
                    ref[s] = part.astype(jnp.bfloat16)
                else:
                    ref[s, :, 0:main] = part[:, 0:main].astype(jnp.bfloat16)
                    ref[s, :, main:wide] = (part[:, main:wide] + ends).astype(jnp.bfloat16)

            return put

        def one(d, total):
            s = peer(d)
            total = pieces(s, put_in(backs[k], s), total)
            back_copy(k, d).start()
            return total

        lanes = main if k == 0 else wide
        none = (jnp.zeros((1, lanes), jnp.float32), jnp.zeros((1, 128), jnp.float32))
        total = lax.fori_loop(1, shards, one, none)
        total = pieces(me, put_in(ins[k], me), total)
        sums[t, 1, k] = jnp.full((8, 128), jnp.sum(total[0]), jnp.float32)
        if k == 1:
            sums[t, 1, 0] = sums[t, 1, 0] + jnp.full((8, 128), jnp.sum(total[1]), jnp.float32)

    start = pl.multiple_of(t * width // 128 * 128, 128)
    shift = t * width - start
    select = shifted(width, TILE, shift)

    def grams(k):
        rows_t = mm(select, grad_t[k, :, pl.ds(start, TILE)], NT).astype(jnp.bfloat16)
        out = []

        @pl.loop(0, side // TILE)
        def _(j):
            at = pl.ds(pl.multiple_of(j * TILE, 128), TILE)
            left[k, :, at] = stat_decay * left[k, :, at] + mm(
                rows_t, grad_t[k, :, at], NN
            ) / MODEL_WIDTH
            right[k, :, at] = stat_decay * right[k, :, at] + mm(
                grad_t[k, t_rows, :], grad_t[k, at, :], NT
            ) / MODEL_WIDTH

        for i, (src, dst) in enumerate(
            ((left, new_left_hbm), (right, new_right_hbm), (moment, new_moment_hbm))
        ):
            copy = pltpu.make_async_copy(src.at[k], dst.at[k], out_sem.at[k, i])
            copy.start()
            out.append(copy)
        return out

    for k in range(slots):
        mirror(k)
    turn_panel(0)
    for k in range(slots):
        pass_on(root_moves[k])
    for copy in stat_in:
        copy.wait()
    moments(0)
    turn_panel(1)

    outs = []
    for k in range(slots):
        pass_on(grad_moves[k])
        for hop in (0, 2):
            grad_moves[k][hop].wait_recv()
        precondition(k)
        if k + 1 < slots:
            moments(k + 1)
            outs += grams(k)

    sum_moves = [
        pltpu.make_async_remote_copy(
            src_ref=sums.at[t],
            dst_ref=sums.at[t],
            send_sem=sum_send.at[i],
            recv_sem=sum_recv.at[i],
            device_id=(me, other),
            device_id_type=MESH,
        )
        for i, other in enumerate((sib, across, diag))
    ]
    for move in sum_moves:
        move.start()
    outs += grams(slots - 1)
    for move in sum_moves:
        move.wait_recv()

    entries = float(MODEL_WIDTH * MODEL_WIDTH)
    totals = sums[0] + sums[1] + sums[2] + sums[3]
    ratio = jnp.sqrt(totals[0] / entries) / jnp.sqrt(totals[1] / entries + graft_eps)
    mine = pl.ds(me * slots, slots)
    ratios[mine] = ratio

    def ratio_copy(d):
        s = peer(d)
        return pltpu.make_async_remote_copy(
            src_ref=ratios.at[mine],
            dst_ref=ratios.at[mine],
            send_sem=rat_send.at[s],
            recv_sem=rat_recv.at[me],
            device_id=(s, t),
            device_id_type=MESH,
        )

    def ratio_arrival(d):
        s = peer(d)
        theirs = pl.ds(s * slots, slots)
        return pltpu.make_async_remote_copy(
            src_ref=ratios.at[theirs],
            dst_ref=ratios.at[theirs],
            send_sem=rat_send.at[s],
            recv_sem=rat_recv.at[s],
            device_id=(s, t),
            device_id_type=MESH,
        )

    @pl.loop(1, shards)
    def _(d):
        ratio_copy(d).start()

    @pl.loop(1, shards)
    def _(d):
        ratio_arrival(d).wait_recv()
        for k in range(slots):
            back_arrival(k, d).wait_recv()

    for b in range(blocks):
        scale = -learn_rate * ratios[slot_of[b]][0:1, 0:1]
        first, second = in_0[owners[b]], in_1[owners[b]]
        at_first = slot_of[b] == owners[b] * slots
        ends = second[:, main:wide].astype(jnp.float32)
        update_ref[b, :, 0:main] = scale * jnp.where(at_first, first, second[:, 0:main]).astype(
            jnp.float32
        )
        update_ref[b, :, main:width] = scale * jnp.where(
            at_first, ends[:, tail : 2 * tail], ends[:, 0:tail]
        )

    @pl.loop(1, shards)
    def _(d):
        ratio_copy(d).wait_send()
        for k in range(slots):
            s1_copy(k, d).wait_send()
            back_copy(k, d).wait_send()

    for k in range(slots):
        for move in root_moves[k] + grad_moves[k]:
            move.wait_send()
    for move in sum_moves:
        move.wait_send()
    for copy in outs:
        copy.wait()


def finish_kernel(weights, update, left, right, moment, weights_out, left_out, right_out, moment_out):
    weights_out[...] = weights[...] + update[...]
    left_out[...] = left[...]
    right_out[...] = right[...]
    moment_out[...] = moment[...]


def kernel_body(
    gradients,
    weights,
    owner_list,
    left_gram_stats,
    right_gram_stats,
    left_root,
    right_root,
    adam_second_moment,
):
    shards = lax.axis_size("shard")
    blocks, rows, width = gradients.shape
    slots = left_gram_stats.shape[0]
    side = rows * shards
    main = width // 128 * 128
    wide = main + 128
    bf16, f32 = jnp.bfloat16, jnp.float32
    flip = lambda a: jnp.transpose(a, (0, 2, 1))
    hbm = pl.BlockSpec(memory_space=pl.ANY)
    vmem = pl.BlockSpec(memory_space=pltpu.VMEM)
    dma = lambda *shape: pltpu.SemaphoreType.DMA(shape)
    stat = jax.ShapeDtypeStruct((slots, width, side), f32)
    update, new_left, new_right, new_moment = pl.pallas_call(
        functools.partial(step_kernel, shards),
        out_shape=(jax.ShapeDtypeStruct((blocks, rows, width), f32), stat, stat, stat),
        in_specs=[pl.BlockSpec(memory_space=pltpu.SMEM), vmem, vmem, hbm, hbm, hbm, hbm],
        out_specs=(vmem, hbm, hbm, hbm),
        scratch_shapes=[
            pltpu.VMEM((shards, rows, wide), bf16),
            pltpu.VMEM((shards, rows, main), bf16),
            pltpu.VMEM((side, wide), bf16),
            pltpu.VMEM((side, main), bf16),
            pltpu.VMEM((slots, side, side), bf16),
            pltpu.VMEM((slots, side, side), bf16),
            pltpu.VMEM((slots, wide, side), bf16),
            pltpu.VMEM((128, side), bf16),
            pltpu.VMEM((shards, rows, main), bf16),
            pltpu.VMEM((shards, rows, wide), bf16),
            pltpu.VMEM((shards, rows, main), bf16),
            pltpu.VMEM((shards, rows, wide), bf16),
            pltpu.VMEM((slots, width, side), f32),
            pltpu.VMEM((slots, width, side), f32),
            pltpu.VMEM((slots, width, side), f32),
            pltpu.VMEM((4, 2, slots, 8, 128), f32),
            pltpu.VMEM((slots * shards, 8, 128), f32),
            dma(slots, shards),
            dma(slots, shards),
            dma(slots, 3),
            dma(slots, 3),
            dma(slots, 3),
            dma(slots, 3),
            dma(slots, shards),
            dma(slots, shards),
            dma(3),
            dma(3),
            dma(shards),
            dma(shards),
            dma(slots + 3),
            dma(slots, 3),
        ],
        compiler_params=pltpu.CompilerParams(
            collective_id=0, has_side_effects=True, vmem_limit_bytes=52 * 2**20
        ),
    )(
        owner_list,
        gradients,
        flip(right_root),
        flip(left_root),
        left_gram_stats,
        right_gram_stats,
        flip(adam_second_moment),
    )
    part = slots * width // blocks
    strip = pl.BlockSpec((1, rows, width), lambda i: (i, 0, 0))
    band = pl.BlockSpec((1, part, side), lambda i: (i * part // width, i % (width // part), 0))
    new_weights, new_left, new_right, new_moment = pl.pallas_call(
        finish_kernel,
        grid=(blocks,),
        out_shape=(jax.ShapeDtypeStruct((blocks, rows, width), f32), stat, stat, stat),
        in_specs=[strip, strip, band, band, band],
        out_specs=(strip, band, band, band),
        compiler_params=pltpu.CompilerParams(vmem_limit_bytes=56 * 2**20),
    )(weights, update, new_left, new_right, new_moment)
    return (new_weights, new_left, new_right, flip(new_moment))


def fits(mesh, gradients, slot_total):
    shards, tensor = mesh.shape["shard"], mesh.shape["tensor"]
    blocks, side, _ = gradients.shape
    rows, width = side // shards, side // tensor
    slots = slot_total // shards
    part = slots * width // blocks
    return (
        tensor == 4
        and slots == 2
        and rows % 16 == 0
        and width % 96 == 0
        and width <= TILE - 96
        and 0 < width % 128 <= 64
        and side % TILE == 0
        and (side // 2) // 128 * 128 % 256 == 0
        and part % 8 == 0
        and width % part == 0
    )


def solution(mesh):
    def run(gradients, *others):
        chosen = kernel_body if fits(mesh, gradients, others[2].shape[0]) else body
        return mapped(chosen)(gradients, *others)

    mapped = lambda chosen: jax.shard_map(
        chosen,
        mesh=mesh,
        in_specs=(
            P(None, "shard", "tensor"),
            P(None, "shard", "tensor"),
            P(),
            P("shard", "tensor", None),
            P("shard", "tensor", None),
            P("shard", None, "tensor"),
            P("shard", None, "tensor"),
            P("shard", None, "tensor"),
        ),
        out_specs=(
            P(None, "shard", "tensor"),
            P("shard", "tensor", None),
            P("shard", "tensor", None),
            P("shard", None, "tensor"),
        ),
        check_vma=False,
    )
    return run
```

```python
import functools

import jax
import jax.numpy as jnp
from jax import lax
from jax.experimental import pallas as pl
from jax.experimental.pallas import tpu as pltpu
from jax.sharding import PartitionSpec as P

MODEL_WIDTH = 1152
SLOTS = 2


stat_decay = 0.95
moment_decay = 0.95
learn_rate = 0.02
graft_eps = 1e-06


def slot_table(owner_list):
    count = owner_list.shape[0]
    positions = jnp.arange(count, dtype=jnp.int32)
    earlier = (owner_list[:, None] == owner_list[None, :]) & (
        positions[None, :] < positions[:, None]
    )
    slot_rank = jnp.sum(earlier.astype(jnp.int32), axis=1)
    return (slot_rank, owner_list * SLOTS + slot_rank)


def body(
    gradients,
    weights,
    owner_list,
    left_gram_stats,
    right_gram_stats,
    left_root,
    right_root,
    adam_second_moment,
):
    shard_count = lax.axis_size("shard")
    tensor_count = lax.axis_size("tensor")
    slots = left_gram_stats.shape[0]
    row_count = gradients.shape[1]
    part_width = gradients.shape[2]
    block_count = owner_list.shape[0]
    slot_rank, slot_index = slot_table(owner_list)
    all_slots = jnp.arange(shard_count * slots, dtype=jnp.int32)
    block_ids = jnp.arange(block_count, dtype=jnp.int32)
    matches = slot_index[None, :] == all_slots[:, None]
    occupied = jnp.any(matches, axis=1)
    source_block = jnp.sum(jnp.where(matches, block_ids[None, :], 0), axis=1)
    outgoing = jnp.where(
        occupied[:, None, None],
        jnp.take(gradients, source_block, axis=0),
        jnp.zeros((), jnp.bfloat16),
    )
    layered = outgoing.reshape(shard_count, 1, slots, row_count, part_width)
    layered = jnp.broadcast_to(layered, (shard_count, tensor_count, slots, row_count, part_width))
    layered = layered.reshape(shard_count * tensor_count * slots, row_count, part_width)
    arrived = lax.all_to_all(layered, ("shard", "tensor"), split_axis=0, concat_axis=0, tiled=True)
    arrived = arrived.reshape(shard_count, tensor_count, slots, row_count, part_width)
    full_grad = jnp.transpose(arrived, (2, 0, 3, 1, 4)).reshape(
        slots, shard_count * row_count, tensor_count * part_width
    )
    tensor_pos = lax.axis_index("tensor")
    own_start = tensor_pos * part_width
    grad_rows = lax.dynamic_slice_in_dim(full_grad, own_start, part_width, 1)
    grad_cols = lax.dynamic_slice_in_dim(full_grad, own_start, part_width, 2)
    gram_left = (
        jnp.einsum("sij,skj->sik", grad_rows, full_grad, preferred_element_type=jnp.float32)
        / MODEL_WIDTH
    )
    gram_right = (
        jnp.einsum("sji,sjk->sik", grad_cols, full_grad, preferred_element_type=jnp.float32)
        / MODEL_WIDTH
    )
    new_left = stat_decay * left_gram_stats + gram_left
    new_right = stat_decay * right_gram_stats + gram_right
    grad_part = grad_cols.astype(jnp.float32)
    new_moment = moment_decay * adam_second_moment + (1.0 - moment_decay) * grad_part * grad_part
    adam_dir = grad_part / jnp.sqrt(new_moment)
    product = jnp.einsum(
        "sij,sjk->sik", full_grad, right_root, preferred_element_type=jnp.float32
    ).astype(jnp.bfloat16)
    precond = jnp.einsum(
        "sij,sjk->sik",
        lax.all_gather(left_root, "tensor", axis=2, tiled=True),
        product,
        preferred_element_type=jnp.float32,
    )
    adam_sum = jnp.sum(adam_dir * adam_dir, axis=(1, 2))
    precond_sum = jnp.sum(precond * precond, axis=(1, 2))
    adam_total, precond_total = lax.psum((adam_sum, precond_sum), "tensor")
    entries = float(MODEL_WIDTH * MODEL_WIDTH)
    ratio = jnp.sqrt(adam_total / entries) / jnp.sqrt(precond_total / entries + graft_eps)
    update = (-learn_rate * ratio)[:, None, None] * precond
    update = update.reshape(slots, shard_count, row_count, part_width)
    returned = lax.all_to_all(update, "shard", split_axis=1, concat_axis=1, tiled=True)
    returned = jnp.transpose(returned, (1, 0, 2, 3)).reshape(
        shard_count * slots, row_count, part_width
    )
    block_update = jnp.take(returned, slot_index, axis=0)
    new_weights = weights + block_update
    return (new_weights, new_left, new_right, new_moment)


MESH = pl.DeviceIdType.MESH
TILE = 384
PIECES = 3
EARLY = 5
NT = (((1,), (1,)), ((), ()))
NN = (((1,), (0,)), ((), ()))


def mm(a, b, dims):
    return lax.dot_general(a, b, dims, preferred_element_type=jnp.float32)


def step_kernel(
    shards,
    owner_ref,
    grad_ref,
    right_root_ref,
    left_root_hbm,
    left_hbm,
    right_hbm,
    moment_hbm,
    update_ref,
    new_left_hbm,
    new_right_hbm,
    new_moment_hbm,
    out_0,
    out_1,
    own_0,
    own_1,
    grad_t,
    left_root,
    prod_t,
    tail_t,
    back_0,
    back_1,
    in_0,
    in_1,
    left,
    right,
    moment,
    sums,
    ratios,
    s1_send,
    s1_recv,
    g_send,
    g_recv,
    l_send,
    l_recv,
    b_send,
    b_recv,
    sum_send,
    sum_recv,
    rat_send,
    rat_recv,
    in_sem,
    out_sem,
):
    me = lax.axis_index("shard")
    t = lax.axis_index("tensor")
    sib = t + 1 - 2 * lax.rem(t, 2)
    across = lax.rem(t + 2, 4)
    diag = lax.rem(sib + 2, 4)
    blocks, rows, width = grad_ref.shape
    side = rows * shards
    slots = left.shape[0]
    main = width // 128 * 128
    tail = width - main
    wide = main + 128
    half = 2 * width
    low, high = half // 128 * 128, -(-half // 128) * 128
    y = t // 2
    out_bufs, owns = (out_0, out_1), (own_0, own_1)
    backs, ins = (back_0, back_1), (in_0, in_1)
    t_rows = pl.ds(pl.multiple_of(t * width, 32), width)
    cut = width // PIECES

    def panel(device, c):
        return pl.ds(pl.multiple_of(device * width + c * cut, 32), cut)


    def peer(d):
        return lax.rem(me + d, shards)

    def strip(s):
        return pl.ds(pl.multiple_of(s * rows, 16), rows)

    root_in = [
        pltpu.make_async_copy(
            left_root_hbm.at[k], left_root.at[k, t_rows, :], in_sem.at[k]
        )
        for k in range(slots)
    ]
    stat_in = [
        pltpu.make_async_copy(src, dst, in_sem.at[slots + i])
        for i, (src, dst) in enumerate(
            ((moment_hbm, moment), (left_hbm, left), (right_hbm, right))
        )
    ]
    for copy in root_in:
        copy.start()

    barrier = pltpu.get_barrier_semaphore()

    @pl.loop(1, shards)
    def _(d):
        pl.semaphore_signal(barrier, inc=1, device_id=(peer(d), t), device_id_type=MESH)

    for other in (sib, across, diag):
        pl.semaphore_signal(barrier, inc=1, device_id=(me, other), device_id_type=MESH)

    owners = [owner_ref[b] for b in range(blocks)]
    slot_of = []
    for b in range(blocks):
        place = owners[b] * slots
        for c in range(b):
            place = place + jnp.where(owners[c] == owners[b], 1, 0)
        slot_of.append(place)

    def pick(k, s):
        source = jnp.int32(0)
        found = jnp.int32(0)
        for b in range(blocks):
            hit = slot_of[b] == s * slots + k
            source = jnp.where(hit, b, source)
            found = jnp.where(hit, 1, found)
        block = grad_ref[source]
        return jnp.where(found > 0, block, jnp.zeros_like(block))

    def shifted(count, lanes, shift):
        row = lax.broadcasted_iota(jnp.int32, (count, lanes), 0)
        col = lax.broadcasted_iota(jnp.int32, (count, lanes), 1)
        return (col == row + shift).astype(jnp.bfloat16)

    def pack(s):
        first, second = pick(0, s), pick(1, s)
        ends = mm(first[:, main:], shifted(tail, 128, 0), NN) + mm(
            second[:, main:], shifted(tail, 128, tail), NN
        )
        return first[:, :main], ends.astype(jnp.bfloat16), second[:, :main]

    pl.semaphore_wait(barrier, shards - 1 + 3)

    def s1_copy(k, d):
        s = peer(d)
        return pltpu.make_async_remote_copy(
            src_ref=out_bufs[k].at[s],
            dst_ref=owns[k].at[strip(me), :],
            send_sem=s1_send.at[k, s],
            recv_sem=s1_recv.at[k, me],
            device_id=(s, t),
            device_id_type=MESH,
        )

    def s1_arrival(k, d):
        s = peer(d)
        return pltpu.make_async_remote_copy(
            src_ref=out_bufs[k].at[s],
            dst_ref=owns[k].at[strip(s), :],
            send_sem=s1_send.at[k, s],
            recv_sem=s1_recv.at[k, s],
            device_id=(s, t),
            device_id_type=MESH,
        )

    def panel_copy(buf, send, recv, k, panel, hop, target, lanes=slice(None)):
        return pltpu.make_async_remote_copy(
            src_ref=buf.at[k, panel, lanes],
            dst_ref=buf.at[k, panel, lanes],
            send_sem=send.at[k, hop],
            recv_sem=recv.at[k, hop],
            device_id=(me, target),
            device_id_type=MESH,
        )

    def window(which):
        return pl.ds(pl.multiple_of(low * which, 128), high)

    def mirror(k):
        root_moves[k][0].wait_recv()
        turn = shifted(half, high, (half - low) * (1 - y))

        @pl.loop(0, low // 256)
        def _(j):
            here = pl.ds(pl.multiple_of(high * y + 256 * j, 128), 256)
            there = pl.ds(pl.multiple_of(half * (1 - y), 32), half)
            piece = left_root[k, here, window(1 - y)]
            left_root[k, there, here] = mm(turn, piece, NT).astype(jnp.bfloat16)

    def root_across(k, c):
        return panel_copy(
            left_root, l_send, l_recv, k, panel(t, c), 1 + c, across, window(y)
        )

    def root_copies(k):
        return (
            panel_copy(left_root, l_send, l_recv, k, t_rows, 0, sib),
            [root_across(k, c) for c in range(PIECES)],
            [
                panel_copy(
                    left_root,
                    l_send,
                    l_recv,
                    k,
                    panel(across, c),
                    1 + PIECES + c,
                    sib,
                    window(1 - y),
                )
                for c in range(PIECES)
            ],
        )

    def grad_copies(k):
        return (
            panel_copy(grad_t, g_send, g_recv, k, t_rows, 0, sib),
            [
                panel_copy(grad_t, g_send, g_recv, k, panel(t, c), 1 + c, across)
                for c in range(PIECES)
            ],
            [
                panel_copy(grad_t, g_send, g_recv, k, panel(across, c), 1 + PIECES + c, sib)
                for c in range(PIECES)
            ],
        )

    root_moves = [root_copies(k) for k in range(slots)]
    grad_moves = [grad_copies(k) for k in range(slots)]

    def send_first(d):
        s = peer(d)
        first, ends, second = pack(s)
        out_0[s, :, 0:main] = first
        out_0[s, :, main:wide] = ends
        out_1[s] = second
        s1_copy(0, d).start()

    for copy in root_in:
        copy.wait()

    @pl.loop(0, slots * PIECES)
    def _(i):
        send_first(i + 1)
        root_across(i // PIECES, lax.rem(i, PIECES)).start()

    for d in range(slots * PIECES + 1, shards):
        send_first(d)
    for k in range(slots):
        root_moves[k][0].start()

    @pl.loop(1, EARLY)
    def _(d):
        s1_copy(1, d).start()

    first, ends, second = pack(me)
    own_0[strip(me), 0:main] = first
    own_0[strip(me), main:wide] = ends
    own_1[strip(me), :] = second
    prod_t[1, width:, :] = jnp.zeros((wide - width, side), jnp.bfloat16)
    tail_t[...] = jnp.zeros((128, side), jnp.bfloat16)
    for copy in stat_in:
        copy.start()

    def turn_panel(k):
        @pl.loop(1, shards)
        def _(d):
            s1_arrival(k, d).wait_recv()

        for j in range(side // TILE):
            at = slice(j * TILE, (j + 1) * TILE)
            if k == 0:
                grad_t[0, t_rows, at] = mm(shifted(width, wide, 0), own_0[at, :], NT).astype(
                    jnp.bfloat16
                )
            else:
                top = pl.ds(pl.multiple_of(t * width, 32), main)
                end = pl.ds(pl.multiple_of(t * width + main, 32), tail)
                grad_t[1, top, at] = mm(shifted(main, main, 0), own_1[at, :], NT).astype(
                    jnp.bfloat16
                )
                grad_t[1, end, at] = mm(
                    shifted(tail, 128, tail), own_0[at, main:wide], NT
                ).astype(jnp.bfloat16)
        for c in range(PIECES):
            grad_moves[k][1][c].start()
            if k == 0 and EARLY + c < shards:
                s1_copy(1, EARLY + c).start()
        grad_moves[k][0].start()

    def pass_on(moves):
        for c in range(PIECES):
            moves[1][c].wait_recv()
            moves[2][c].start()

    def arrived(moves):
        for c in range(PIECES):
            moves[2][c].wait_recv()

    chunk = 96

    def moments(k):
        def one(j, total):
            at = pl.ds(pl.multiple_of(j * chunk, 32), chunk)
            g = grad_t[k, pl.ds(pl.multiple_of(t * width + j * chunk, 32), chunk), :].astype(
                jnp.float32
            )
            fresh = moment_decay * moment[k, at, :] + (1.0 - moment_decay) * g * g
            moment[k, at, :] = fresh
            direction = g / jnp.sqrt(fresh)
            return total + jnp.sum(direction * direction, axis=0, keepdims=True)

        total = lax.fori_loop(0, width // chunk, one, jnp.zeros((1, side), jnp.float32))
        sums[t, 0, k] = jnp.full((8, 128), jnp.sum(total), jnp.float32)

    def back_copy(k, d):
        s = peer(d)
        return pltpu.make_async_remote_copy(
            src_ref=backs[k].at[s],
            dst_ref=ins[k].at[me],
            send_sem=b_send.at[k, s],
            recv_sem=b_recv.at[k, me],
            device_id=(s, t),
            device_id_type=MESH,
        )

    def back_arrival(k, d):
        s = peer(d)
        return pltpu.make_async_remote_copy(
            src_ref=backs[k].at[s],
            dst_ref=ins[k].at[s],
            send_sem=b_send.at[k, s],
            recv_sem=b_recv.at[k, s],
            device_id=(s, t),
            device_id_type=MESH,
        )

    def precondition(k):
        @pl.loop(0, side // TILE)
        def _(j):
            at = pl.ds(pl.multiple_of(j * TILE, 128), TILE)
            prod_t[k, 0:width, at] = mm(right_root_ref[k], grad_t[k, :, at], NN).astype(
                jnp.bfloat16
            )

        if k == 0:
            tail_t[tail : 2 * tail, :] = prod_t[0, main:width, :]
        arrived(root_moves[k])

        def squares(part):
            return jnp.sum(part * part, axis=0, keepdims=True)

        def pieces(s, put, total):
            if k == 0:
                part = mm(left_root[0, strip(s), :], prod_t[0, 0:main, :], NT)
                put(part)
                return total[0] + squares(part), total[1]
            part = mm(left_root[1, strip(s), :], prod_t[1], NT)
            ends = mm(left_root[0, strip(s), :], tail_t[...], NT)
            put(part, ends)
            return total[0] + squares(part), total[1] + squares(ends)

        def put_in(ref, s):
            def put(part, ends=None):
                if ends is None:
                    ref[s] = part.astype(jnp.bfloat16)
                else:
                    ref[s, :, 0:main] = part[:, 0:main].astype(jnp.bfloat16)
                    ref[s, :, main:wide] = (part[:, main:wide] + ends).astype(jnp.bfloat16)

            return put

        def one(d, total):
            s = peer(d)
            total = pieces(s, put_in(backs[k], s), total)
            back_copy(k, d).start()
            return total

        def hold(d, total):
            s = peer(d)
            return pieces(s, put_in(backs[k], s), total)

        lanes = main if k == 0 else wide
        none = (jnp.zeros((1, lanes), jnp.float32), jnp.zeros((1, 128), jnp.float32))
        if k == 0:
            total = lax.fori_loop(1, EARLY, one, none)
            total = lax.fori_loop(EARLY, shards, hold, total)
        else:
            total = lax.fori_loop(1, shards, one, none)
        total = pieces(me, put_in(ins[k], me), total)
        sums[t, 1, k] = jnp.full((8, 128), jnp.sum(total[0]), jnp.float32)
        if k == 1:
            sums[t, 1, 0] = sums[t, 1, 0] + jnp.full((8, 128), jnp.sum(total[1]), jnp.float32)

    start = pl.multiple_of(t * width // 128 * 128, 128)
    shift = t * width - start
    select = shifted(width, TILE, shift)

    def grams(k):
        rows_t = mm(select, grad_t[k, :, pl.ds(start, TILE)], NT).astype(jnp.bfloat16)
        out = []

        @pl.loop(0, side // TILE)
        def _(j):
            at = pl.ds(pl.multiple_of(j * TILE, 128), TILE)
            left[k, :, at] = stat_decay * left[k, :, at] + mm(
                rows_t, grad_t[k, :, at], NN
            ) / MODEL_WIDTH
            right[k, :, at] = stat_decay * right[k, :, at] + mm(
                grad_t[k, t_rows, :], grad_t[k, at, :], NT
            ) / MODEL_WIDTH

        for i, (src, dst) in enumerate(
            ((left, new_left_hbm), (right, new_right_hbm), (moment, new_moment_hbm))
        ):
            copy = pltpu.make_async_copy(src.at[k], dst.at[k], out_sem.at[k, i])
            copy.start()
            out.append(copy)
        return out

    for k in range(slots):
        mirror(k)
    turn_panel(0)
    for k in range(slots):
        pass_on(root_moves[k])
    for copy in stat_in:
        copy.wait()
    moments(0)
    turn_panel(1)

    outs = []
    for k in range(slots):
        pass_on(grad_moves[k])
        if k == 1:
            for d in range(EARLY, shards):
                back_copy(0, d).start()
        grad_moves[k][0].wait_recv()
        arrived(grad_moves[k])
        precondition(k)
        if k + 1 < slots:
            moments(k + 1)
            outs += grams(k)

    sum_moves = [
        pltpu.make_async_remote_copy(
            src_ref=sums.at[t],
            dst_ref=sums.at[t],
            send_sem=sum_send.at[i],
            recv_sem=sum_recv.at[i],
            device_id=(me, other),
            device_id_type=MESH,
        )
        for i, other in enumerate((sib, across, diag))
    ]
    for move in sum_moves:
        move.start()
    outs += grams(slots - 1)
    for move in sum_moves:
        move.wait_recv()

    entries = float(MODEL_WIDTH * MODEL_WIDTH)
    totals = sums[0] + sums[1] + sums[2] + sums[3]
    ratio = jnp.sqrt(totals[0] / entries) / jnp.sqrt(totals[1] / entries + graft_eps)
    mine = pl.ds(me * slots, slots)
    ratios[mine] = ratio

    def ratio_copy(d):
        s = peer(d)
        return pltpu.make_async_remote_copy(
            src_ref=ratios.at[mine],
            dst_ref=ratios.at[mine],
            send_sem=rat_send.at[s],
            recv_sem=rat_recv.at[me],
            device_id=(s, t),
            device_id_type=MESH,
        )

    def ratio_arrival(d):
        s = peer(d)
        theirs = pl.ds(s * slots, slots)
        return pltpu.make_async_remote_copy(
            src_ref=ratios.at[theirs],
            dst_ref=ratios.at[theirs],
            send_sem=rat_send.at[s],
            recv_sem=rat_recv.at[s],
            device_id=(s, t),
            device_id_type=MESH,
        )

    @pl.loop(1, shards)
    def _(d):
        ratio_copy(d).start()

    @pl.loop(1, shards)
    def _(d):
        ratio_arrival(d).wait_recv()
        for k in range(slots):
            back_arrival(k, d).wait_recv()

    for b in range(blocks):
        scale = -learn_rate * ratios[slot_of[b]][0:1, 0:1]
        first, second = in_0[owners[b]], in_1[owners[b]]
        at_first = slot_of[b] == owners[b] * slots
        ends = second[:, main:wide].astype(jnp.float32)
        update_ref[b, :, 0:main] = scale * jnp.where(at_first, first, second[:, 0:main]).astype(
            jnp.float32
        )
        update_ref[b, :, main:width] = scale * jnp.where(
            at_first, ends[:, tail : 2 * tail], ends[:, 0:tail]
        )

    @pl.loop(1, shards)
    def _(d):
        ratio_copy(d).wait_send()
        for k in range(slots):
            s1_copy(k, d).wait_send()
            back_copy(k, d).wait_send()

    for k in range(slots):
        for moves in (root_moves[k], grad_moves[k]):
            for move in [moves[0]] + moves[1] + moves[2]:
                move.wait_send()
    for move in sum_moves:
        move.wait_send()
    for copy in outs:
        copy.wait()


def finish_kernel(
    weights, update, left, right, moment, weights_out, left_out, right_out, moment_out, sem
):
    copies = [
        pltpu.make_async_copy(src.at[k], dst.at[k], sem.at[i, k])
        for i, (src, dst) in enumerate(((left, left_out), (right, right_out), (moment, moment_out)))
        for k in range(src.shape[0])
    ]
    for copy in copies:
        copy.start()
    weights_out[...] = weights[...] + update[...]
    for copy in copies:
        copy.wait()


def kernel_body(
    gradients,
    weights,
    owner_list,
    left_gram_stats,
    right_gram_stats,
    left_root,
    right_root,
    adam_second_moment,
):
    shards = lax.axis_size("shard")
    blocks, rows, width = gradients.shape
    slots = left_gram_stats.shape[0]
    side = rows * shards
    main = width // 128 * 128
    wide = main + 128
    bf16, f32 = jnp.bfloat16, jnp.float32
    flip = lambda a: jnp.transpose(a, (0, 2, 1))
    hbm = pl.BlockSpec(memory_space=pl.ANY)
    vmem = pl.BlockSpec(memory_space=pltpu.VMEM)
    dma = lambda *shape: pltpu.SemaphoreType.DMA(shape)
    stat = jax.ShapeDtypeStruct((slots, width, side), f32)
    update, new_left, new_right, new_moment = pl.pallas_call(
        functools.partial(step_kernel, shards),
        out_shape=(jax.ShapeDtypeStruct((blocks, rows, width), f32), stat, stat, stat),
        in_specs=[pl.BlockSpec(memory_space=pltpu.SMEM), vmem, vmem, hbm, hbm, hbm, hbm],
        out_specs=(vmem, hbm, hbm, hbm),
        scratch_shapes=[
            pltpu.VMEM((shards, rows, wide), bf16),
            pltpu.VMEM((shards, rows, main), bf16),
            pltpu.VMEM((side, wide), bf16),
            pltpu.VMEM((side, main), bf16),
            pltpu.VMEM((slots, side, side), bf16),
            pltpu.VMEM((slots, side, side), bf16),
            pltpu.VMEM((slots, wide, side), bf16),
            pltpu.VMEM((128, side), bf16),
            pltpu.VMEM((shards, rows, main), bf16),
            pltpu.VMEM((shards, rows, wide), bf16),
            pltpu.VMEM((shards, rows, main), bf16),
            pltpu.VMEM((shards, rows, wide), bf16),
            pltpu.VMEM((slots, width, side), f32),
            pltpu.VMEM((slots, width, side), f32),
            pltpu.VMEM((slots, width, side), f32),
            pltpu.VMEM((4, 2, slots, 8, 128), f32),
            pltpu.VMEM((slots * shards, 8, 128), f32),
            dma(slots, shards),
            dma(slots, shards),
            dma(slots, 1 + 2 * PIECES),
            dma(slots, 1 + 2 * PIECES),
            dma(slots, 1 + 2 * PIECES),
            dma(slots, 1 + 2 * PIECES),
            dma(slots, shards),
            dma(slots, shards),
            dma(3),
            dma(3),
            dma(shards),
            dma(shards),
            dma(slots + 3),
            dma(slots, 3),
        ],
        compiler_params=pltpu.CompilerParams(
            collective_id=0, has_side_effects=True, vmem_limit_bytes=52 * 2**20
        ),
    )(
        owner_list,
        gradients,
        flip(right_root),
        flip(left_root),
        left_gram_stats,
        right_gram_stats,
        flip(adam_second_moment),
    )
    new_weights, new_left, new_right, new_moment = pl.pallas_call(
        finish_kernel,
        out_shape=(jax.ShapeDtypeStruct((blocks, rows, width), f32), stat, stat, stat),
        in_specs=[vmem, vmem, hbm, hbm, hbm],
        out_specs=(vmem, hbm, hbm, hbm),
        scratch_shapes=[dma(3, slots)],
        compiler_params=pltpu.CompilerParams(vmem_limit_bytes=56 * 2**20),
    )(weights, update, new_left, new_right, new_moment)
    return (new_weights, new_left, new_right, flip(new_moment))


def fits(mesh, gradients, slot_total):
    shards, tensor = mesh.shape["shard"], mesh.shape["tensor"]
    blocks, side, _ = gradients.shape
    rows, width = side // shards, side // tensor
    slots = slot_total // shards
    part = slots * width // blocks
    return (
        tensor == 4
        and slots == 2
        and rows % 16 == 0
        and width % 96 == 0
        and width // PIECES % 32 == 0
        and slots * PIECES < shards <= EARLY + PIECES
        and EARLY < shards
        and width <= TILE - 96
        and 0 < width % 128 <= 64
        and side % TILE == 0
        and (side // 2) // 128 * 128 % 256 == 0
        and part % 8 == 0
        and width % part == 0
    )


def solution(mesh):
    def run(gradients, *others):
        chosen = kernel_body if fits(mesh, gradients, others[2].shape[0]) else body
        return mapped(chosen)(gradients, *others)

    mapped = lambda chosen: jax.shard_map(
        chosen,
        mesh=mesh,
        in_specs=(
            P(None, "shard", "tensor"),
            P(None, "shard", "tensor"),
            P(),
            P("shard", "tensor", None),
            P("shard", "tensor", None),
            P("shard", None, "tensor"),
            P("shard", None, "tensor"),
            P("shard", None, "tensor"),
        ),
        out_specs=(
            P(None, "shard", "tensor"),
            P("shard", "tensor", None),
            P("shard", "tensor", None),
            P("shard", None, "tensor"),
        ),
        check_vma=False,
    )
    return run
```

```python
import functools

import jax
import jax.numpy as jnp
from jax import lax
from jax.experimental import pallas as pl
from jax.experimental.pallas import tpu as pltpu
from jax.sharding import PartitionSpec as P

MODEL_WIDTH = 1152
SLOTS = 2


stat_decay = 0.95
moment_decay = 0.95
learn_rate = 0.02
graft_eps = 1e-06


def slot_table(owner_list):
    count = owner_list.shape[0]
    positions = jnp.arange(count, dtype=jnp.int32)
    earlier = (owner_list[:, None] == owner_list[None, :]) & (
        positions[None, :] < positions[:, None]
    )
    slot_rank = jnp.sum(earlier.astype(jnp.int32), axis=1)
    return (slot_rank, owner_list * SLOTS + slot_rank)


def body(
    gradients,
    weights,
    owner_list,
    left_gram_stats,
    right_gram_stats,
    left_root,
    right_root,
    adam_second_moment,
):
    shard_count = lax.axis_size("shard")
    tensor_count = lax.axis_size("tensor")
    slots = left_gram_stats.shape[0]
    row_count = gradients.shape[1]
    part_width = gradients.shape[2]
    block_count = owner_list.shape[0]
    slot_rank, slot_index = slot_table(owner_list)
    all_slots = jnp.arange(shard_count * slots, dtype=jnp.int32)
    block_ids = jnp.arange(block_count, dtype=jnp.int32)
    matches = slot_index[None, :] == all_slots[:, None]
    occupied = jnp.any(matches, axis=1)
    source_block = jnp.sum(jnp.where(matches, block_ids[None, :], 0), axis=1)
    outgoing = jnp.where(
        occupied[:, None, None],
        jnp.take(gradients, source_block, axis=0),
        jnp.zeros((), jnp.bfloat16),
    )
    layered = outgoing.reshape(shard_count, 1, slots, row_count, part_width)
    layered = jnp.broadcast_to(layered, (shard_count, tensor_count, slots, row_count, part_width))
    layered = layered.reshape(shard_count * tensor_count * slots, row_count, part_width)
    arrived = lax.all_to_all(layered, ("shard", "tensor"), split_axis=0, concat_axis=0, tiled=True)
    arrived = arrived.reshape(shard_count, tensor_count, slots, row_count, part_width)
    full_grad = jnp.transpose(arrived, (2, 0, 3, 1, 4)).reshape(
        slots, shard_count * row_count, tensor_count * part_width
    )
    tensor_pos = lax.axis_index("tensor")
    own_start = tensor_pos * part_width
    grad_rows = lax.dynamic_slice_in_dim(full_grad, own_start, part_width, 1)
    grad_cols = lax.dynamic_slice_in_dim(full_grad, own_start, part_width, 2)
    gram_left = (
        jnp.einsum("sij,skj->sik", grad_rows, full_grad, preferred_element_type=jnp.float32)
        / MODEL_WIDTH
    )
    gram_right = (
        jnp.einsum("sji,sjk->sik", grad_cols, full_grad, preferred_element_type=jnp.float32)
        / MODEL_WIDTH
    )
    new_left = stat_decay * left_gram_stats + gram_left
    new_right = stat_decay * right_gram_stats + gram_right
    grad_part = grad_cols.astype(jnp.float32)
    new_moment = moment_decay * adam_second_moment + (1.0 - moment_decay) * grad_part * grad_part
    adam_dir = grad_part / jnp.sqrt(new_moment)
    product = jnp.einsum(
        "sij,sjk->sik", full_grad, right_root, preferred_element_type=jnp.float32
    ).astype(jnp.bfloat16)
    precond = jnp.einsum(
        "sij,sjk->sik",
        lax.all_gather(left_root, "tensor", axis=2, tiled=True),
        product,
        preferred_element_type=jnp.float32,
    )
    adam_sum = jnp.sum(adam_dir * adam_dir, axis=(1, 2))
    precond_sum = jnp.sum(precond * precond, axis=(1, 2))
    adam_total, precond_total = lax.psum((adam_sum, precond_sum), "tensor")
    entries = float(MODEL_WIDTH * MODEL_WIDTH)
    ratio = jnp.sqrt(adam_total / entries) / jnp.sqrt(precond_total / entries + graft_eps)
    update = (-learn_rate * ratio)[:, None, None] * precond
    update = update.reshape(slots, shard_count, row_count, part_width)
    returned = lax.all_to_all(update, "shard", split_axis=1, concat_axis=1, tiled=True)
    returned = jnp.transpose(returned, (1, 0, 2, 3)).reshape(
        shard_count * slots, row_count, part_width
    )
    block_update = jnp.take(returned, slot_index, axis=0)
    new_weights = weights + block_update
    return (new_weights, new_left, new_right, new_moment)


MESH = pl.DeviceIdType.MESH
TILE = 384
NT = (((1,), (1,)), ((), ()))
NN = (((1,), (0,)), ((), ()))


def mm(a, b, dims):
    return lax.dot_general(a, b, dims, preferred_element_type=jnp.float32)


def step_kernel(
    shards,
    owner_hbm,
    grad_hbm,
    right_root_hbm,
    left_root_hbm,
    left_hbm,
    right_hbm,
    moment_hbm,
    in_0,
    in_1,
    ratios,
    left,
    right,
    moment,
    out_0,
    out_1,
    own_0,
    own_1,
    grad_t,
    left_root,
    prod_t,
    tail_t,
    back_0,
    back_1,
    sums,
    owner_ref,
    grad_ref,
    right_root_ref,
    s1_send,
    s1_recv,
    g_send,
    g_recv,
    l_send,
    l_recv,
    b_send,
    b_recv,
    sum_send,
    sum_recv,
    rat_send,
    rat_recv,
    in_sem,
    own_sem,
):
    me = lax.axis_index("shard")
    t = lax.axis_index("tensor")
    sib = t + 1 - 2 * lax.rem(t, 2)
    across = lax.rem(t + 2, 4)
    diag = lax.rem(sib + 2, 4)
    blocks, rows, width = grad_ref.shape
    side = rows * shards
    slots = left.shape[0]
    main = width // 128 * 128
    tail = width - main
    wide = main + 128
    half = 2 * width
    low, high = half // 128 * 128, -(-half // 128) * 128
    y = t // 2
    out_bufs, owns = (out_0, out_1), (own_0, own_1)
    backs, ins = (back_0, back_1), (in_0, in_1)
    t_rows = pl.ds(pl.multiple_of(t * width, 32), width)
    across_rows = pl.ds(pl.multiple_of(across * width, 32), width)

    def peer(d):
        return lax.rem(me + d, shards)

    def strip(s):
        return pl.ds(pl.multiple_of(s * rows, 16), rows)

    root_in = [
        pltpu.make_async_copy(
            left_root_hbm.at[k], left_root.at[k, t_rows, :], in_sem.at[k]
        )
        for k in range(slots)
    ]
    stat_in = [
        pltpu.make_async_copy(src, dst, in_sem.at[slots + i])
        for i, (src, dst) in enumerate(
            ((moment_hbm, moment), (left_hbm, left), (right_hbm, right))
        )
    ]
    first_in = [
        pltpu.make_async_copy(src, dst, in_sem.at[slots + 3 + i])
        for i, (src, dst) in enumerate(
            ((owner_hbm, owner_ref), (grad_hbm, grad_ref), (right_root_hbm, right_root_ref))
        )
    ]
    for copy in first_in + root_in:
        copy.start()

    barrier = pltpu.get_barrier_semaphore()

    @pl.loop(1, shards)
    def _(d):
        pl.semaphore_signal(barrier, inc=1, device_id=(peer(d), t), device_id_type=MESH)

    for other in (sib, across, diag):
        pl.semaphore_signal(barrier, inc=1, device_id=(me, other), device_id_type=MESH)

    first_in[0].wait()

    owners = [owner_ref[b] for b in range(blocks)]
    slot_of = []
    for b in range(blocks):
        place = owners[b] * slots
        for c in range(b):
            place = place + jnp.where(owners[c] == owners[b], 1, 0)
        slot_of.append(place)

    def pick(k, s):
        source = jnp.int32(0)
        found = jnp.int32(0)
        for b in range(blocks):
            hit = slot_of[b] == s * slots + k
            source = jnp.where(hit, b, source)
            found = jnp.where(hit, 1, found)
        block = grad_ref[source]
        return jnp.where(found > 0, block, jnp.zeros_like(block))

    def shifted(count, lanes, shift):
        row = lax.broadcasted_iota(jnp.int32, (count, lanes), 0)
        col = lax.broadcasted_iota(jnp.int32, (count, lanes), 1)
        return (col == row + shift).astype(jnp.bfloat16)

    def pack(s):
        first, second = pick(0, s), pick(1, s)
        ends = mm(first[:, main:], shifted(tail, 128, 0), NN) + mm(
            second[:, main:], shifted(tail, 128, tail), NN
        )
        return first[:, :main], ends.astype(jnp.bfloat16), second[:, :main]

    first_in[1].wait()
    pl.semaphore_wait(barrier, shards - 1 + 3)

    def s1_copy(k, d):
        s = peer(d)
        return pltpu.make_async_remote_copy(
            src_ref=out_bufs[k].at[s],
            dst_ref=owns[k].at[strip(me), :],
            send_sem=s1_send.at[k, s],
            recv_sem=s1_recv.at[k, me],
            device_id=(s, t),
            device_id_type=MESH,
        )

    def s1_arrival(k, d):
        s = peer(d)
        return pltpu.make_async_remote_copy(
            src_ref=out_bufs[k].at[s],
            dst_ref=owns[k].at[strip(s), :],
            send_sem=s1_send.at[k, s],
            recv_sem=s1_recv.at[k, s],
            device_id=(s, t),
            device_id_type=MESH,
        )

    def panel_copy(buf, send, recv, k, panel, hop, target, lanes=slice(None)):
        return pltpu.make_async_remote_copy(
            src_ref=buf.at[k, panel, lanes],
            dst_ref=buf.at[k, panel, lanes],
            send_sem=send.at[k, hop],
            recv_sem=recv.at[k, hop],
            device_id=(me, target),
            device_id_type=MESH,
        )

    def window(which):
        return pl.ds(pl.multiple_of(low * which, 128), high)

    def mirror(k):
        root_moves[k][0].wait_recv()
        turn = shifted(half, high, (half - low) * (1 - y))

        @pl.loop(0, low // 256)
        def _(j):
            here = pl.ds(pl.multiple_of(high * y + 256 * j, 128), 256)
            there = pl.ds(pl.multiple_of(half * (1 - y), 32), half)
            piece = left_root[k, here, window(1 - y)]
            left_root[k, there, here] = mm(turn, piece, NT).astype(jnp.bfloat16)

    def root_copies(k):
        return (
            panel_copy(left_root, l_send, l_recv, k, t_rows, 0, sib),
            panel_copy(left_root, l_send, l_recv, k, t_rows, 1, across, window(y)),
            panel_copy(left_root, l_send, l_recv, k, across_rows, 2, sib, window(1 - y)),
        )

    def grad_copies(k):
        return (
            panel_copy(grad_t, g_send, g_recv, k, t_rows, 0, sib),
            panel_copy(grad_t, g_send, g_recv, k, t_rows, 1, across),
            panel_copy(grad_t, g_send, g_recv, k, across_rows, 2, sib),
        )

    root_moves = [root_copies(k) for k in range(slots)]
    grad_moves = [grad_copies(k) for k in range(slots)]

    @pl.loop(1, shards)
    def _(d):
        s = peer(d)
        first, ends, second = pack(s)
        out_0[s, :, 0:main] = first
        out_0[s, :, main:wide] = ends
        out_1[s] = second
        s1_copy(0, d).start()

    for k in range(slots):
        root_in[k].wait()
        root_moves[k][1].start()
        root_moves[k][0].start()

    @pl.loop(1, shards)
    def _(d):
        s1_copy(1, d).start()

    first, ends, second = pack(me)
    own_0[strip(me), 0:main] = first
    own_0[strip(me), main:wide] = ends
    own_1[strip(me), :] = second
    prod_t[1, width:, :] = jnp.zeros((wide - width, side), jnp.bfloat16)
    tail_t[...] = jnp.zeros((128, side), jnp.bfloat16)
    for copy in stat_in:
        copy.start()

    def turn_panel(k):
        @pl.loop(1, shards)
        def _(d):
            s1_arrival(k, d).wait_recv()

        for j in range(side // TILE):
            at = slice(j * TILE, (j + 1) * TILE)
            if k == 0:
                grad_t[0, t_rows, at] = mm(shifted(width, wide, 0), own_0[at, :], NT).astype(
                    jnp.bfloat16
                )
            else:
                top = pl.ds(pl.multiple_of(t * width, 32), main)
                end = pl.ds(pl.multiple_of(t * width + main, 32), tail)
                grad_t[1, top, at] = mm(shifted(main, main, 0), own_1[at, :], NT).astype(
                    jnp.bfloat16
                )
                grad_t[1, end, at] = mm(
                    shifted(tail, 128, tail), own_0[at, main:wide], NT
                ).astype(jnp.bfloat16)
        grad_moves[k][1].start()
        grad_moves[k][0].start()

    def pass_on(moves):
        moves[1].wait_recv()
        moves[2].start()

    chunk = 96

    def moments(k):
        def one(j, total):
            at = pl.ds(pl.multiple_of(j * chunk, 32), chunk)
            g = grad_t[k, pl.ds(pl.multiple_of(t * width + j * chunk, 32), chunk), :].astype(
                jnp.float32
            )
            fresh = moment_decay * moment[k, at, :] + (1.0 - moment_decay) * g * g
            moment[k, at, :] = fresh
            direction = g / jnp.sqrt(fresh)
            return total + jnp.sum(direction * direction, axis=0, keepdims=True)

        total = lax.fori_loop(0, width // chunk, one, jnp.zeros((1, side), jnp.float32))
        sums[t, 0, k] = jnp.full((8, 128), jnp.sum(total), jnp.float32)

    def back_copy(k, s):
        return pltpu.make_async_remote_copy(
            src_ref=backs[k].at[s],
            dst_ref=ins[k].at[me],
            send_sem=b_send.at[k, s],
            recv_sem=b_recv.at[k, me],
            device_id=(s, t),
            device_id_type=MESH,
        )

    own_copies = [
        pltpu.make_async_copy(backs[k].at[me], ins[k].at[me], own_sem.at[k]) for k in range(slots)
    ]

    def back_arrival(k, d):
        s = peer(d)
        return pltpu.make_async_remote_copy(
            src_ref=backs[k].at[s],
            dst_ref=ins[k].at[s],
            send_sem=b_send.at[k, s],
            recv_sem=b_recv.at[k, s],
            device_id=(s, t),
            device_id_type=MESH,
        )

    def precondition(k):
        @pl.loop(0, side // TILE)
        def _(j):
            at = pl.ds(pl.multiple_of(j * TILE, 128), TILE)
            prod_t[k, 0:width, at] = mm(right_root_ref[k], grad_t[k, :, at], NN).astype(
                jnp.bfloat16
            )

        if k == 0:
            tail_t[tail : 2 * tail, :] = prod_t[0, main:width, :]
        root_moves[k][2].wait_recv()

        group = shards // 2
        lanes = main if k == 0 else wide
        squares, end_squares = jnp.zeros((1, lanes), jnp.float32), jnp.zeros((1, 128), jnp.float32)
        for turn in range(2):
            first = lax.rem(me // group + 1 + turn, 2) * group
            band = pl.ds(pl.multiple_of(first * rows, 32), group * rows)
            part = mm(left_root[k, band, :], prod_t[k, 0:lanes, :], NT)
            squares += jnp.sum(part * part, axis=0, keepdims=True)
            if k == 1:
                ends = mm(left_root[0, band, :], tail_t[...], NT)
                end_squares += jnp.sum(ends * ends, axis=0, keepdims=True)
            for j in range(group):
                piece = part[j * rows : (j + 1) * rows]
                if k == 0:
                    back_0[first + j] = piece.astype(jnp.bfloat16)
                else:
                    back_1[first + j, :, 0:main] = piece[:, 0:main].astype(jnp.bfloat16)
                    back_1[first + j, :, main:wide] = (
                        piece[:, main:wide] + ends[j * rows : (j + 1) * rows]
                    ).astype(jnp.bfloat16)
            for j in range(group):
                s = first + lax.rem(lax.rem(me, group) + 1 + j, group)
                if turn == 1 and j == group - 1:
                    own_copies[k].start()
                else:
                    back_copy(k, s).start()
        total = (squares, end_squares)
        sums[t, 1, k] = jnp.full((8, 128), jnp.sum(total[0]), jnp.float32)
        if k == 1:
            sums[t, 1, 0] = sums[t, 1, 0] + jnp.full((8, 128), jnp.sum(total[1]), jnp.float32)

    start = pl.multiple_of(t * width // 128 * 128, 128)
    shift = t * width - start
    select = shifted(width, TILE, shift)

    def grams(k):
        rows_t = mm(select, grad_t[k, :, pl.ds(start, TILE)], NT).astype(jnp.bfloat16)

        @pl.loop(0, side // TILE)
        def _(j):
            at = pl.ds(pl.multiple_of(j * TILE, 128), TILE)
            left[k, :, at] = stat_decay * left[k, :, at] + mm(
                rows_t, grad_t[k, :, at], NN
            ) / MODEL_WIDTH
            right[k, :, at] = stat_decay * right[k, :, at] + mm(
                grad_t[k, t_rows, :], grad_t[k, at, :], NT
            ) / MODEL_WIDTH


    for k in range(slots):
        mirror(k)
    first_in[2].wait()
    turn_panel(0)
    for k in range(slots):
        pass_on(root_moves[k])
    for copy in stat_in:
        copy.wait()
    moments(0)
    turn_panel(1)

    for k in range(slots):
        pass_on(grad_moves[k])
        for hop in (0, 2):
            grad_moves[k][hop].wait_recv()
        precondition(k)
        if k + 1 < slots:
            moments(k + 1)
            grams(k)

    sum_moves = [
        pltpu.make_async_remote_copy(
            src_ref=sums.at[t],
            dst_ref=sums.at[t],
            send_sem=sum_send.at[i],
            recv_sem=sum_recv.at[i],
            device_id=(me, other),
            device_id_type=MESH,
        )
        for i, other in enumerate((sib, across, diag))
    ]
    for move in sum_moves:
        move.start()
    grams(slots - 1)
    for move in sum_moves:
        move.wait_recv()

    entries = float(MODEL_WIDTH * MODEL_WIDTH)
    totals = sums[0] + sums[1] + sums[2] + sums[3]
    ratio = jnp.sqrt(totals[0] / entries) / jnp.sqrt(totals[1] / entries + graft_eps)
    mine = pl.ds(me * slots, slots)
    ratios[mine] = ratio

    def ratio_copy(d):
        s = peer(d)
        return pltpu.make_async_remote_copy(
            src_ref=ratios.at[mine],
            dst_ref=ratios.at[mine],
            send_sem=rat_send.at[s],
            recv_sem=rat_recv.at[me],
            device_id=(s, t),
            device_id_type=MESH,
        )

    def ratio_arrival(d):
        s = peer(d)
        theirs = pl.ds(s * slots, slots)
        return pltpu.make_async_remote_copy(
            src_ref=ratios.at[theirs],
            dst_ref=ratios.at[theirs],
            send_sem=rat_send.at[s],
            recv_sem=rat_recv.at[s],
            device_id=(s, t),
            device_id_type=MESH,
        )

    @pl.loop(1, shards)
    def _(d):
        ratio_copy(d).start()

    @pl.loop(1, shards)
    def _(d):
        ratio_arrival(d).wait_recv()
        for k in range(slots):
            back_arrival(k, d).wait_recv()

    @pl.loop(1, shards)
    def _(d):
        ratio_copy(d).wait_send()
        for k in range(slots):
            s1_copy(k, d).wait_send()
            back_copy(k, peer(d)).wait_send()

    for k in range(slots):
        for move in root_moves[k] + grad_moves[k]:
            move.wait_send()
    for move in sum_moves:
        move.wait_send()
    for copy in own_copies:
        copy.wait()


def finish_kernel(
    owners,
    weights,
    first,
    second,
    ratios,
    left,
    right,
    moment,
    weights_out,
    left_out,
    right_out,
    moment_out,
    sem,
):
    copies = [
        pltpu.make_async_copy(src.at[k], dst.at[k], sem.at[i, k])
        for i, (src, dst) in enumerate(((left, left_out), (right, right_out), (moment, moment_out)))
        for k in range(src.shape[0])
    ]
    for copy in copies:
        copy.start()
    blocks, _, width = weights.shape
    main = first.shape[2]
    tail = width - main
    for b in range(blocks):
        rank = jnp.int32(0)
        for c in range(b):
            rank = rank + jnp.where(owners[c] == owners[b], 1, 0)
        scale = -learn_rate * ratios[owners[b] * SLOTS + rank][0:1, 0:1]
        other = second[owners[b]]
        whole = jnp.where(rank == 0, first[owners[b]], other[:, 0:main]).astype(jnp.float32)
        ends = other[:, main:].astype(jnp.float32)
        ends = jnp.where(rank == 0, ends[:, tail : 2 * tail], ends[:, 0:tail])
        weights_out[b, :, 0:main] = weights[b, :, 0:main] + scale * whole
        weights_out[b, :, main:] = weights[b, :, main:] + scale * ends
    for copy in copies:
        copy.wait()


def kernel_body(
    gradients,
    weights,
    owner_list,
    left_gram_stats,
    right_gram_stats,
    left_root,
    right_root,
    adam_second_moment,
):
    shards = lax.axis_size("shard")
    blocks, rows, width = gradients.shape
    slots = left_gram_stats.shape[0]
    side = rows * shards
    main = width // 128 * 128
    wide = main + 128
    bf16, f32 = jnp.bfloat16, jnp.float32
    flip = lambda a: jnp.transpose(a, (0, 2, 1))
    hbm = pl.BlockSpec(memory_space=pl.ANY)
    vmem = pl.BlockSpec(memory_space=pltpu.VMEM)
    dma = lambda *shape: pltpu.SemaphoreType.DMA(shape)
    stat = jax.ShapeDtypeStruct((slots, width, side), f32)
    first, second, ratios, new_left, new_right, new_moment = pl.pallas_call(
        functools.partial(step_kernel, shards),
        out_shape=(
            jax.ShapeDtypeStruct((shards, rows, main), bf16),
            jax.ShapeDtypeStruct((shards, rows, wide), bf16),
            jax.ShapeDtypeStruct((slots * shards, 8, 128), f32),
            stat,
            stat,
            stat,
        ),
        in_specs=[pl.BlockSpec(memory_space=pltpu.HBM)] * 7,
        out_specs=(hbm, hbm, vmem, vmem, vmem, vmem),
        scratch_shapes=[
            pltpu.VMEM((shards, rows, wide), bf16),
            pltpu.VMEM((shards, rows, main), bf16),
            pltpu.VMEM((side, wide), bf16),
            pltpu.VMEM((side, main), bf16),
            pltpu.VMEM((slots, side, side), bf16),
            pltpu.VMEM((slots, side, side), bf16),
            pltpu.VMEM((slots, wide, side), bf16),
            pltpu.VMEM((128, side), bf16),
            pltpu.VMEM((shards, rows, main), bf16),
            pltpu.VMEM((shards, rows, wide), bf16),
            pltpu.VMEM((4, 2, slots, 8, 128), f32),
            pltpu.SMEM((blocks,), jnp.int32),
            pltpu.VMEM((blocks, rows, width), bf16),
            pltpu.VMEM((slots, width, side), bf16),
            dma(slots, shards),
            dma(slots, shards),
            dma(slots, 3),
            dma(slots, 3),
            dma(slots, 3),
            dma(slots, 3),
            dma(slots, shards),
            dma(slots, shards),
            dma(3),
            dma(3),
            dma(shards),
            dma(shards),
            dma(slots + 6),
            dma(slots),
        ],
        compiler_params=pltpu.CompilerParams(
            collective_id=0, has_side_effects=True, vmem_limit_bytes=40 * 2**20
        ),
    )(
        owner_list,
        gradients,
        flip(right_root),
        flip(left_root),
        left_gram_stats,
        right_gram_stats,
        flip(adam_second_moment),
    )
    new_weights, new_left, new_right, new_moment = pl.pallas_call(
        finish_kernel,
        in_specs=[pl.BlockSpec(memory_space=pltpu.SMEM)] + [vmem] * 7,
        out_specs=(vmem, hbm, hbm, hbm),
        out_shape=(jax.ShapeDtypeStruct((blocks, rows, width), f32), stat, stat, stat),
        scratch_shapes=[dma(3, slots)],
        compiler_params=pltpu.CompilerParams(vmem_limit_bytes=24 * 2**20),
    )(owner_list, weights, first, second, ratios, new_left, new_right, new_moment)
    return (new_weights, new_left, new_right, flip(new_moment))


def fits(mesh, gradients, slot_total):
    shards, tensor = mesh.shape["shard"], mesh.shape["tensor"]
    blocks, side, _ = gradients.shape
    rows, width = side // shards, side // tensor
    slots = slot_total // shards
    part = slots * width // blocks
    return (
        tensor == 4
        and slots == 2
        and rows % 16 == 0
        and shards % 2 == 0
        and rows * shards // 2 % 32 == 0
        and width % 96 == 0
        and width <= TILE - 96
        and 0 < width % 128 <= 64
        and side % TILE == 0
        and (side // 2) // 128 * 128 % 256 == 0
        and part % 8 == 0
        and width % part == 0
    )


def solution(mesh):
    def run(gradients, *others):
        chosen = kernel_body if fits(mesh, gradients, others[2].shape[0]) else body
        return mapped(chosen)(gradients, *others)

    mapped = lambda chosen: jax.shard_map(
        chosen,
        mesh=mesh,
        in_specs=(
            P(None, "shard", "tensor"),
            P(None, "shard", "tensor"),
            P(),
            P("shard", "tensor", None),
            P("shard", "tensor", None),
            P("shard", None, "tensor"),
            P("shard", None, "tensor"),
            P("shard", None, "tensor"),
        ),
        out_specs=(
            P(None, "shard", "tensor"),
            P("shard", "tensor", None),
            P("shard", "tensor", None),
            P("shard", None, "tensor"),
        ),
        check_vma=False,
    )
    return run
```

```python
import functools

import jax
import jax.numpy as jnp
from jax import lax
from jax.experimental import pallas as pl
from jax.experimental.pallas import tpu as pltpu
from jax.sharding import PartitionSpec as P

MODEL_WIDTH = 1152
SLOTS = 2


stat_decay = 0.95
moment_decay = 0.95
learn_rate = 0.02
graft_eps = 1e-06


def slot_table(owner_list):
    count = owner_list.shape[0]
    positions = jnp.arange(count, dtype=jnp.int32)
    earlier = (owner_list[:, None] == owner_list[None, :]) & (
        positions[None, :] < positions[:, None]
    )
    slot_rank = jnp.sum(earlier.astype(jnp.int32), axis=1)
    return (slot_rank, owner_list * SLOTS + slot_rank)


def body(
    gradients,
    weights,
    owner_list,
    left_gram_stats,
    right_gram_stats,
    left_root,
    right_root,
    adam_second_moment,
):
    shard_count = lax.axis_size("shard")
    tensor_count = lax.axis_size("tensor")
    slots = left_gram_stats.shape[0]
    row_count = gradients.shape[1]
    part_width = gradients.shape[2]
    block_count = owner_list.shape[0]
    slot_rank, slot_index = slot_table(owner_list)
    all_slots = jnp.arange(shard_count * slots, dtype=jnp.int32)
    block_ids = jnp.arange(block_count, dtype=jnp.int32)
    matches = slot_index[None, :] == all_slots[:, None]
    occupied = jnp.any(matches, axis=1)
    source_block = jnp.sum(jnp.where(matches, block_ids[None, :], 0), axis=1)
    outgoing = jnp.where(
        occupied[:, None, None],
        jnp.take(gradients, source_block, axis=0),
        jnp.zeros((), jnp.bfloat16),
    )
    layered = outgoing.reshape(shard_count, 1, slots, row_count, part_width)
    layered = jnp.broadcast_to(layered, (shard_count, tensor_count, slots, row_count, part_width))
    layered = layered.reshape(shard_count * tensor_count * slots, row_count, part_width)
    arrived = lax.all_to_all(layered, ("shard", "tensor"), split_axis=0, concat_axis=0, tiled=True)
    arrived = arrived.reshape(shard_count, tensor_count, slots, row_count, part_width)
    full_grad = jnp.transpose(arrived, (2, 0, 3, 1, 4)).reshape(
        slots, shard_count * row_count, tensor_count * part_width
    )
    tensor_pos = lax.axis_index("tensor")
    own_start = tensor_pos * part_width
    grad_rows = lax.dynamic_slice_in_dim(full_grad, own_start, part_width, 1)
    grad_cols = lax.dynamic_slice_in_dim(full_grad, own_start, part_width, 2)
    gram_left = (
        jnp.einsum("sij,skj->sik", grad_rows, full_grad, preferred_element_type=jnp.float32)
        / MODEL_WIDTH
    )
    gram_right = (
        jnp.einsum("sji,sjk->sik", grad_cols, full_grad, preferred_element_type=jnp.float32)
        / MODEL_WIDTH
    )
    new_left = stat_decay * left_gram_stats + gram_left
    new_right = stat_decay * right_gram_stats + gram_right
    grad_part = grad_cols.astype(jnp.float32)
    new_moment = moment_decay * adam_second_moment + (1.0 - moment_decay) * grad_part * grad_part
    adam_dir = grad_part / jnp.sqrt(new_moment)
    product = jnp.einsum(
        "sij,sjk->sik", full_grad, right_root, preferred_element_type=jnp.float32
    ).astype(jnp.bfloat16)
    precond = jnp.einsum(
        "sij,sjk->sik",
        lax.all_gather(left_root, "tensor", axis=2, tiled=True),
        product,
        preferred_element_type=jnp.float32,
    )
    adam_sum = jnp.sum(adam_dir * adam_dir, axis=(1, 2))
    precond_sum = jnp.sum(precond * precond, axis=(1, 2))
    adam_total, precond_total = lax.psum((adam_sum, precond_sum), "tensor")
    entries = float(MODEL_WIDTH * MODEL_WIDTH)
    ratio = jnp.sqrt(adam_total / entries) / jnp.sqrt(precond_total / entries + graft_eps)
    update = (-learn_rate * ratio)[:, None, None] * precond
    update = update.reshape(slots, shard_count, row_count, part_width)
    returned = lax.all_to_all(update, "shard", split_axis=1, concat_axis=1, tiled=True)
    returned = jnp.transpose(returned, (1, 0, 2, 3)).reshape(
        shard_count * slots, row_count, part_width
    )
    block_update = jnp.take(returned, slot_index, axis=0)
    new_weights = weights + block_update
    return (new_weights, new_left, new_right, new_moment)


MESH = pl.DeviceIdType.MESH
TILE = 384
NT = (((1,), (1,)), ((), ()))
NN = (((1,), (0,)), ((), ()))


def mm(a, b, dims):
    return lax.dot_general(a, b, dims, preferred_element_type=jnp.float32)


def step_kernel(
    shards,
    owner_hbm,
    grad_hbm,
    right_root_hbm,
    left_root_hbm,
    left_hbm,
    right_hbm,
    moment_hbm,
    in_0,
    in_1,
    ratios,
    left,
    right,
    moment,
    out_0,
    out_1,
    own_0,
    own_1,
    grad_t,
    left_root,
    prod_t,
    tail_t,
    back_0,
    back_1,
    sums,
    owner_ref,
    grad_ref,
    right_root_ref,
    s1_send,
    s1_recv,
    g_send,
    g_recv,
    l_send,
    l_recv,
    b_send,
    b_recv,
    sum_send,
    sum_recv,
    rat_send,
    rat_recv,
    in_sem,
    own_sem,
):
    me = lax.axis_index("shard")
    t = lax.axis_index("tensor")
    sib = t + 1 - 2 * lax.rem(t, 2)
    across = lax.rem(t + 2, 4)
    diag = lax.rem(sib + 2, 4)
    blocks, rows, width = grad_ref.shape
    side = rows * shards
    slots = left.shape[0]
    main = width // 128 * 128
    tail = width - main
    wide = main + 128
    half = 2 * width
    low, high = half // 128 * 128, -(-half // 128) * 128
    y = t // 2
    out_bufs, owns = (out_0, out_1), (own_0, own_1)
    backs, ins = (back_0, back_1), (in_0, in_1)
    t_rows = pl.ds(pl.multiple_of(t * width, 32), width)
    across_rows = pl.ds(pl.multiple_of(across * width, 32), width)

    group = shards // 2

    def peer(d):
        far = jnp.where(d <= group, 1, 0)
        return lax.rem(me // group + far, 2) * group + lax.rem(me + d, group)

    def strip(s):
        return pl.ds(pl.multiple_of(s * rows, 16), rows)

    root_in = [
        pltpu.make_async_copy(
            left_root_hbm.at[k], left_root.at[k, t_rows, :], in_sem.at[k]
        )
        for k in range(slots)
    ]
    stat_in = [
        pltpu.make_async_copy(src, dst, in_sem.at[slots + i])
        for i, (src, dst) in enumerate(
            ((moment_hbm, moment), (left_hbm, left), (right_hbm, right))
        )
    ]
    first_in = [
        pltpu.make_async_copy(src, dst, in_sem.at[slots + 3 + i])
        for i, (src, dst) in enumerate(
            ((owner_hbm, owner_ref), (grad_hbm, grad_ref), (right_root_hbm, right_root_ref))
        )
    ]
    for copy in first_in + root_in:
        copy.start()

    barrier = pltpu.get_barrier_semaphore()

    @pl.loop(1, shards)
    def _(d):
        pl.semaphore_signal(barrier, inc=1, device_id=(peer(d), t), device_id_type=MESH)

    for other in (sib, across, diag):
        pl.semaphore_signal(barrier, inc=1, device_id=(me, other), device_id_type=MESH)

    first_in[0].wait()

    owners = [owner_ref[b] for b in range(blocks)]
    slot_of = []
    for b in range(blocks):
        place = owners[b] * slots
        for c in range(b):
            place = place + jnp.where(owners[c] == owners[b], 1, 0)
        slot_of.append(place)

    def pick(k, s):
        source = jnp.int32(0)
        found = jnp.int32(0)
        for b in range(blocks):
            hit = slot_of[b] == s * slots + k
            source = jnp.where(hit, b, source)
            found = jnp.where(hit, 1, found)
        block = grad_ref[source]
        return jnp.where(found > 0, block, jnp.zeros_like(block))

    def shifted(count, lanes, shift):
        row = lax.broadcasted_iota(jnp.int32, (count, lanes), 0)
        col = lax.broadcasted_iota(jnp.int32, (count, lanes), 1)
        return (col == row + shift).astype(jnp.bfloat16)

    def pack(s):
        first, second = pick(0, s), pick(1, s)
        ends = mm(first[:, main:], shifted(tail, 128, 0), NN) + mm(
            second[:, main:], shifted(tail, 128, tail), NN
        )
        return first[:, :main], ends.astype(jnp.bfloat16), second[:, :main]

    first_in[1].wait()
    pl.semaphore_wait(barrier, shards - 1 + 3)

    def s1_copy(k, d):
        s = peer(d)
        return pltpu.make_async_remote_copy(
            src_ref=out_bufs[k].at[s],
            dst_ref=owns[k].at[strip(me), :],
            send_sem=s1_send.at[k, s],
            recv_sem=s1_recv.at[k, me],
            device_id=(s, t),
            device_id_type=MESH,
        )

    def s1_arrival(k, d):
        s = peer(d)
        return pltpu.make_async_remote_copy(
            src_ref=out_bufs[k].at[s],
            dst_ref=owns[k].at[strip(s), :],
            send_sem=s1_send.at[k, s],
            recv_sem=s1_recv.at[k, s],
            device_id=(s, t),
            device_id_type=MESH,
        )

    def panel_copy(buf, send, recv, k, panel, hop, target, lanes=slice(None)):
        return pltpu.make_async_remote_copy(
            src_ref=buf.at[k, panel, lanes],
            dst_ref=buf.at[k, panel, lanes],
            send_sem=send.at[k, hop],
            recv_sem=recv.at[k, hop],
            device_id=(me, target),
            device_id_type=MESH,
        )

    def window(which):
        return pl.ds(pl.multiple_of(low * which, 128), high)

    def mirror(k):
        root_moves[k][0].wait_recv()
        turn = shifted(half, high, (half - low) * (1 - y))

        @pl.loop(0, low // 256)
        def _(j):
            here = pl.ds(pl.multiple_of(high * y + 256 * j, 128), 256)
            there = pl.ds(pl.multiple_of(half * (1 - y), 32), half)
            piece = left_root[k, here, window(1 - y)]
            left_root[k, there, here] = mm(turn, piece, NT).astype(jnp.bfloat16)

    def root_copies(k):
        return (
            panel_copy(left_root, l_send, l_recv, k, t_rows, 0, sib),
            panel_copy(left_root, l_send, l_recv, k, t_rows, 1, across, window(y)),
            panel_copy(left_root, l_send, l_recv, k, across_rows, 2, sib, window(1 - y)),
        )

    def grad_copies(k):
        return (
            panel_copy(grad_t, g_send, g_recv, k, t_rows, 0, sib),
            panel_copy(grad_t, g_send, g_recv, k, t_rows, 1, across),
            panel_copy(grad_t, g_send, g_recv, k, across_rows, 2, sib),
        )

    root_moves = [root_copies(k) for k in range(slots)]
    grad_moves = [grad_copies(k) for k in range(slots)]

    @pl.loop(1, shards)
    def _(d):
        s = peer(d)
        first, ends, second = pack(s)
        out_0[s, :, 0:main] = first
        out_0[s, :, main:wide] = ends
        out_1[s] = second
        s1_copy(0, d).start()

    for k in range(slots):
        root_in[k].wait()
        root_moves[k][1].start()
        root_moves[k][0].start()

    @pl.loop(1, shards)
    def _(d):
        s1_copy(1, d).start()

    first, ends, second = pack(me)
    own_0[strip(me), 0:main] = first
    own_0[strip(me), main:wide] = ends
    own_1[strip(me), :] = second
    prod_t[1, width:, :] = jnp.zeros((wide - width, side), jnp.bfloat16)
    tail_t[...] = jnp.zeros((128, side), jnp.bfloat16)
    for copy in stat_in:
        copy.start()

    def turn_panel(k):
        @pl.loop(1, shards)
        def _(d):
            s1_arrival(k, d).wait_recv()

        for j in range(side // TILE):
            at = slice(j * TILE, (j + 1) * TILE)
            if k == 0:
                grad_t[0, t_rows, at] = mm(shifted(width, wide, 0), own_0[at, :], NT).astype(
                    jnp.bfloat16
                )
            else:
                top = pl.ds(pl.multiple_of(t * width, 32), main)
                end = pl.ds(pl.multiple_of(t * width + main, 32), tail)
                grad_t[1, top, at] = mm(shifted(main, main, 0), own_1[at, :], NT).astype(
                    jnp.bfloat16
                )
                grad_t[1, end, at] = mm(
                    shifted(tail, 128, tail), own_0[at, main:wide], NT
                ).astype(jnp.bfloat16)
        grad_moves[k][1].start()
        grad_moves[k][0].start()

    def pass_on(moves):
        moves[1].wait_recv()
        moves[2].start()

    chunk = 96

    def moments(k):
        def one(j, total):
            at = pl.ds(pl.multiple_of(j * chunk, 32), chunk)
            g = grad_t[k, pl.ds(pl.multiple_of(t * width + j * chunk, 32), chunk), :].astype(
                jnp.float32
            )
            fresh = moment_decay * moment[k, at, :] + (1.0 - moment_decay) * g * g
            moment[k, at, :] = fresh
            direction = g / jnp.sqrt(fresh)
            return total + jnp.sum(direction * direction, axis=0, keepdims=True)

        total = lax.fori_loop(0, width // chunk, one, jnp.zeros((1, side), jnp.float32))
        sums[t, 0, k] = jnp.full((8, 128), jnp.sum(total), jnp.float32)

    def back_copy(k, s):
        return pltpu.make_async_remote_copy(
            src_ref=backs[k].at[s],
            dst_ref=ins[k].at[me],
            send_sem=b_send.at[k, s],
            recv_sem=b_recv.at[k, me],
            device_id=(s, t),
            device_id_type=MESH,
        )

    own_copies = [
        pltpu.make_async_copy(backs[k].at[me], ins[k].at[me], own_sem.at[k]) for k in range(slots)
    ]

    def back_arrival(k, d):
        s = peer(d)
        return pltpu.make_async_remote_copy(
            src_ref=backs[k].at[s],
            dst_ref=ins[k].at[s],
            send_sem=b_send.at[k, s],
            recv_sem=b_recv.at[k, s],
            device_id=(s, t),
            device_id_type=MESH,
        )

    def precondition(k):
        @pl.loop(0, side // TILE)
        def _(j):
            at = pl.ds(pl.multiple_of(j * TILE, 128), TILE)
            prod_t[k, 0:width, at] = mm(right_root_ref[k], grad_t[k, :, at], NN).astype(
                jnp.bfloat16
            )

        if k == 0:
            tail_t[tail : 2 * tail, :] = prod_t[0, main:width, :]
        root_moves[k][2].wait_recv()

        lanes = main if k == 0 else wide
        squares, end_squares = jnp.zeros((1, lanes), jnp.float32), jnp.zeros((1, 128), jnp.float32)
        for turn in range(2):
            first = lax.rem(me // group + 1 + turn, 2) * group
            band = pl.ds(pl.multiple_of(first * rows, 32), group * rows)
            part = mm(left_root[k, band, :], prod_t[k, 0:lanes, :], NT)
            squares += jnp.sum(part * part, axis=0, keepdims=True)
            if k == 1:
                ends = mm(left_root[0, band, :], tail_t[...], NT)
                end_squares += jnp.sum(ends * ends, axis=0, keepdims=True)
            for j in range(group):
                piece = part[j * rows : (j + 1) * rows]
                if k == 0:
                    back_0[first + j] = piece.astype(jnp.bfloat16)
                else:
                    back_1[first + j, :, 0:main] = piece[:, 0:main].astype(jnp.bfloat16)
                    back_1[first + j, :, main:wide] = (
                        piece[:, main:wide] + ends[j * rows : (j + 1) * rows]
                    ).astype(jnp.bfloat16)
            for j in range(group):
                s = first + lax.rem(lax.rem(me, group) + 1 + j, group)
                if turn == 1 and j == group - 1:
                    own_copies[k].start()
                else:
                    back_copy(k, s).start()
        total = (squares, end_squares)
        sums[t, 1, k] = jnp.full((8, 128), jnp.sum(total[0]), jnp.float32)
        if k == 1:
            sums[t, 1, 0] = sums[t, 1, 0] + jnp.full((8, 128), jnp.sum(total[1]), jnp.float32)

    start = pl.multiple_of(t * width // 128 * 128, 128)
    shift = t * width - start
    select = shifted(width, TILE, shift)

    def grams(k):
        rows_t = mm(select, grad_t[k, :, pl.ds(start, TILE)], NT).astype(jnp.bfloat16)

        @pl.loop(0, side // TILE)
        def _(j):
            at = pl.ds(pl.multiple_of(j * TILE, 128), TILE)
            left[k, :, at] = stat_decay * left[k, :, at] + mm(
                rows_t, grad_t[k, :, at], NN
            ) / MODEL_WIDTH
            right[k, :, at] = stat_decay * right[k, :, at] + mm(
                grad_t[k, t_rows, :], grad_t[k, at, :], NT
            ) / MODEL_WIDTH


    for k in range(slots):
        mirror(k)
    first_in[2].wait()
    turn_panel(0)
    for k in range(slots):
        pass_on(root_moves[k])
    for copy in stat_in:
        copy.wait()
    moments(0)
    turn_panel(1)

    for k in range(slots):
        pass_on(grad_moves[k])
        for hop in (0, 2):
            grad_moves[k][hop].wait_recv()
        precondition(k)
        if k + 1 < slots:
            moments(k + 1)
            grams(k)

    sum_moves = [
        pltpu.make_async_remote_copy(
            src_ref=sums.at[t],
            dst_ref=sums.at[t],
            send_sem=sum_send.at[i],
            recv_sem=sum_recv.at[i],
            device_id=(me, other),
            device_id_type=MESH,
        )
        for i, other in enumerate((sib, across, diag))
    ]
    for move in sum_moves:
        move.start()
    grams(slots - 1)
    for move in sum_moves:
        move.wait_recv()

    entries = float(MODEL_WIDTH * MODEL_WIDTH)
    totals = sums[0] + sums[1] + sums[2] + sums[3]
    ratio = jnp.sqrt(totals[0] / entries) / jnp.sqrt(totals[1] / entries + graft_eps)
    mine = pl.ds(me * slots, slots)
    ratios[mine] = ratio

    def ratio_copy(d):
        s = peer(d)
        return pltpu.make_async_remote_copy(
            src_ref=ratios.at[mine],
            dst_ref=ratios.at[mine],
            send_sem=rat_send.at[s],
            recv_sem=rat_recv.at[me],
            device_id=(s, t),
            device_id_type=MESH,
        )

    def ratio_arrival(d):
        s = peer(d)
        theirs = pl.ds(s * slots, slots)
        return pltpu.make_async_remote_copy(
            src_ref=ratios.at[theirs],
            dst_ref=ratios.at[theirs],
            send_sem=rat_send.at[s],
            recv_sem=rat_recv.at[s],
            device_id=(s, t),
            device_id_type=MESH,
        )

    @pl.loop(1, shards)
    def _(d):
        ratio_copy(d).start()

    @pl.loop(1, shards)
    def _(d):
        ratio_arrival(d).wait_recv()
        for k in range(slots):
            back_arrival(k, d).wait_recv()

    @pl.loop(1, shards)
    def _(d):
        ratio_copy(d).wait_send()
        for k in range(slots):
            s1_copy(k, d).wait_send()
            back_copy(k, peer(d)).wait_send()

    for k in range(slots):
        for move in root_moves[k] + grad_moves[k]:
            move.wait_send()
    for move in sum_moves:
        move.wait_send()
    for copy in own_copies:
        copy.wait()


def finish_kernel(
    owners,
    weights,
    first,
    second,
    ratios,
    left,
    right,
    moment,
    weights_out,
    left_out,
    right_out,
    moment_out,
    sem,
):
    copies = [
        pltpu.make_async_copy(src.at[k], dst.at[k], sem.at[i, k])
        for i, (src, dst) in enumerate(((left, left_out), (right, right_out), (moment, moment_out)))
        for k in range(src.shape[0])
    ]
    for copy in copies:
        copy.start()
    blocks, _, width = weights.shape
    main = first.shape[2]
    tail = width - main
    for b in range(blocks):
        rank = jnp.int32(0)
        for c in range(b):
            rank = rank + jnp.where(owners[c] == owners[b], 1, 0)
        scale = -learn_rate * ratios[owners[b] * SLOTS + rank][0:1, 0:1]
        other = second[owners[b]]
        whole = jnp.where(rank == 0, first[owners[b]], other[:, 0:main]).astype(jnp.float32)
        ends = other[:, main:].astype(jnp.float32)
        ends = jnp.where(rank == 0, ends[:, tail : 2 * tail], ends[:, 0:tail])
        weights_out[b, :, 0:main] = weights[b, :, 0:main] + scale * whole
        weights_out[b, :, main:] = weights[b, :, main:] + scale * ends
    for copy in copies:
        copy.wait()


def kernel_body(
    gradients,
    weights,
    owner_list,
    left_gram_stats,
    right_gram_stats,
    left_root,
    right_root,
    adam_second_moment,
):
    shards = lax.axis_size("shard")
    blocks, rows, width = gradients.shape
    slots = left_gram_stats.shape[0]
    side = rows * shards
    main = width // 128 * 128
    wide = main + 128
    bf16, f32 = jnp.bfloat16, jnp.float32
    flip = lambda a: jnp.transpose(a, (0, 2, 1))
    hbm = pl.BlockSpec(memory_space=pl.ANY)
    vmem = pl.BlockSpec(memory_space=pltpu.VMEM)
    dma = lambda *shape: pltpu.SemaphoreType.DMA(shape)
    stat = jax.ShapeDtypeStruct((slots, width, side), f32)
    first, second, ratios, new_left, new_right, new_moment = pl.pallas_call(
        functools.partial(step_kernel, shards),
        out_shape=(
            jax.ShapeDtypeStruct((shards, rows, main), bf16),
            jax.ShapeDtypeStruct((shards, rows, wide), bf16),
            jax.ShapeDtypeStruct((slots * shards, 8, 128), f32),
            stat,
            stat,
            stat,
        ),
        in_specs=[pl.BlockSpec(memory_space=pltpu.HBM)] * 7,
        out_specs=(hbm, hbm, vmem, vmem, vmem, vmem),
        scratch_shapes=[
            pltpu.VMEM((shards, rows, wide), bf16),
            pltpu.VMEM((shards, rows, main), bf16),
            pltpu.VMEM((side, wide), bf16),
            pltpu.VMEM((side, main), bf16),
            pltpu.VMEM((slots, side, side), bf16),
            pltpu.VMEM((slots, side, side), bf16),
            pltpu.VMEM((slots, wide, side), bf16),
            pltpu.VMEM((128, side), bf16),
            pltpu.VMEM((shards, rows, main), bf16),
            pltpu.VMEM((shards, rows, wide), bf16),
            pltpu.VMEM((4, 2, slots, 8, 128), f32),
            pltpu.SMEM((blocks,), jnp.int32),
            pltpu.VMEM((blocks, rows, width), bf16),
            pltpu.VMEM((slots, width, side), bf16),
            dma(slots, shards),
            dma(slots, shards),
            dma(slots, 3),
            dma(slots, 3),
            dma(slots, 3),
            dma(slots, 3),
            dma(slots, shards),
            dma(slots, shards),
            dma(3),
            dma(3),
            dma(shards),
            dma(shards),
            dma(slots + 6),
            dma(slots),
        ],
        compiler_params=pltpu.CompilerParams(
            collective_id=0, has_side_effects=True, vmem_limit_bytes=40 * 2**20
        ),
    )(
        owner_list,
        gradients,
        flip(right_root),
        flip(left_root),
        left_gram_stats,
        right_gram_stats,
        flip(adam_second_moment),
    )
    new_weights, new_left, new_right, new_moment = pl.pallas_call(
        finish_kernel,
        in_specs=[pl.BlockSpec(memory_space=pltpu.SMEM)] + [vmem] * 7,
        out_specs=(vmem, hbm, hbm, hbm),
        out_shape=(jax.ShapeDtypeStruct((blocks, rows, width), f32), stat, stat, stat),
        scratch_shapes=[dma(3, slots)],
        compiler_params=pltpu.CompilerParams(vmem_limit_bytes=24 * 2**20),
    )(owner_list, weights, first, second, ratios, new_left, new_right, new_moment)
    return (new_weights, new_left, new_right, flip(new_moment))


def fits(mesh, gradients, slot_total):
    shards, tensor = mesh.shape["shard"], mesh.shape["tensor"]
    blocks, side, _ = gradients.shape
    rows, width = side // shards, side // tensor
    slots = slot_total // shards
    part = slots * width // blocks
    return (
        tensor == 4
        and slots == 2
        and rows % 16 == 0
        and shards % 2 == 0
        and rows * shards // 2 % 32 == 0
        and width % 96 == 0
        and width <= TILE - 96
        and 0 < width % 128 <= 64
        and side % TILE == 0
        and (side // 2) // 128 * 128 % 256 == 0
        and part % 8 == 0
        and width % part == 0
    )


def solution(mesh):
    def run(gradients, *others):
        chosen = kernel_body if fits(mesh, gradients, others[2].shape[0]) else body
        return mapped(chosen)(gradients, *others)

    mapped = lambda chosen: jax.shard_map(
        chosen,
        mesh=mesh,
        in_specs=(
            P(None, "shard", "tensor"),
            P(None, "shard", "tensor"),
            P(),
            P("shard", "tensor", None),
            P("shard", "tensor", None),
            P("shard", None, "tensor"),
            P("shard", None, "tensor"),
            P("shard", None, "tensor"),
        ),
        out_specs=(
            P(None, "shard", "tensor"),
            P("shard", "tensor", None),
            P("shard", "tensor", None),
            P("shard", None, "tensor"),
        ),
        check_vma=False,
    )
    return run
```

```python
import functools

import jax
import jax.numpy as jnp
from jax import lax
from jax.experimental import pallas as pl
from jax.experimental.pallas import tpu as pltpu
from jax.sharding import PartitionSpec as P

MODEL_WIDTH = 1152
SLOTS = 2


stat_decay = 0.95
moment_decay = 0.95
learn_rate = 0.02
graft_eps = 1e-06


def slot_table(owner_list):
    count = owner_list.shape[0]
    positions = jnp.arange(count, dtype=jnp.int32)
    earlier = (owner_list[:, None] == owner_list[None, :]) & (
        positions[None, :] < positions[:, None]
    )
    slot_rank = jnp.sum(earlier.astype(jnp.int32), axis=1)
    return (slot_rank, owner_list * SLOTS + slot_rank)


def body(
    gradients,
    weights,
    owner_list,
    left_gram_stats,
    right_gram_stats,
    left_root,
    right_root,
    adam_second_moment,
):
    shard_count = lax.axis_size("shard")
    tensor_count = lax.axis_size("tensor")
    slots = left_gram_stats.shape[0]
    row_count = gradients.shape[1]
    part_width = gradients.shape[2]
    block_count = owner_list.shape[0]
    slot_rank, slot_index = slot_table(owner_list)
    all_slots = jnp.arange(shard_count * slots, dtype=jnp.int32)
    block_ids = jnp.arange(block_count, dtype=jnp.int32)
    matches = slot_index[None, :] == all_slots[:, None]
    occupied = jnp.any(matches, axis=1)
    source_block = jnp.sum(jnp.where(matches, block_ids[None, :], 0), axis=1)
    outgoing = jnp.where(
        occupied[:, None, None],
        jnp.take(gradients, source_block, axis=0),
        jnp.zeros((), jnp.bfloat16),
    )
    layered = outgoing.reshape(shard_count, 1, slots, row_count, part_width)
    layered = jnp.broadcast_to(layered, (shard_count, tensor_count, slots, row_count, part_width))
    layered = layered.reshape(shard_count * tensor_count * slots, row_count, part_width)
    arrived = lax.all_to_all(layered, ("shard", "tensor"), split_axis=0, concat_axis=0, tiled=True)
    arrived = arrived.reshape(shard_count, tensor_count, slots, row_count, part_width)
    full_grad = jnp.transpose(arrived, (2, 0, 3, 1, 4)).reshape(
        slots, shard_count * row_count, tensor_count * part_width
    )
    tensor_pos = lax.axis_index("tensor")
    own_start = tensor_pos * part_width
    grad_rows = lax.dynamic_slice_in_dim(full_grad, own_start, part_width, 1)
    grad_cols = lax.dynamic_slice_in_dim(full_grad, own_start, part_width, 2)
    gram_left = (
        jnp.einsum("sij,skj->sik", grad_rows, full_grad, preferred_element_type=jnp.float32)
        / MODEL_WIDTH
    )
    gram_right = (
        jnp.einsum("sji,sjk->sik", grad_cols, full_grad, preferred_element_type=jnp.float32)
        / MODEL_WIDTH
    )
    new_left = stat_decay * left_gram_stats + gram_left
    new_right = stat_decay * right_gram_stats + gram_right
    grad_part = grad_cols.astype(jnp.float32)
    new_moment = moment_decay * adam_second_moment + (1.0 - moment_decay) * grad_part * grad_part
    adam_dir = grad_part / jnp.sqrt(new_moment)
    product = jnp.einsum(
        "sij,sjk->sik", full_grad, right_root, preferred_element_type=jnp.float32
    ).astype(jnp.bfloat16)
    precond = jnp.einsum(
        "sij,sjk->sik",
        lax.all_gather(left_root, "tensor", axis=2, tiled=True),
        product,
        preferred_element_type=jnp.float32,
    )
    adam_sum = jnp.sum(adam_dir * adam_dir, axis=(1, 2))
    precond_sum = jnp.sum(precond * precond, axis=(1, 2))
    adam_total, precond_total = lax.psum((adam_sum, precond_sum), "tensor")
    entries = float(MODEL_WIDTH * MODEL_WIDTH)
    ratio = jnp.sqrt(adam_total / entries) / jnp.sqrt(precond_total / entries + graft_eps)
    update = (-learn_rate * ratio)[:, None, None] * precond
    update = update.reshape(slots, shard_count, row_count, part_width)
    returned = lax.all_to_all(update, "shard", split_axis=1, concat_axis=1, tiled=True)
    returned = jnp.transpose(returned, (1, 0, 2, 3)).reshape(
        shard_count * slots, row_count, part_width
    )
    block_update = jnp.take(returned, slot_index, axis=0)
    new_weights = weights + block_update
    return (new_weights, new_left, new_right, new_moment)


MESH = pl.DeviceIdType.MESH
TILE = 384
NT = (((1,), (1,)), ((), ()))
NN = (((1,), (0,)), ((), ()))


def mm(a, b, dims):
    return lax.dot_general(a, b, dims, preferred_element_type=jnp.float32)


def step_kernel(
    shards,
    owner_hbm,
    grad_hbm,
    right_root_hbm,
    left_root_hbm,
    left_hbm,
    right_hbm,
    moment_hbm,
    in_0,
    in_1,
    ratios,
    left,
    right,
    moment,
    out_0,
    out_1,
    own_0,
    own_1,
    grad_t,
    left_root,
    prod_t,
    tail_t,
    back_0,
    back_1,
    sums,
    owner_ref,
    grad_ref,
    right_root_ref,
    s1_send,
    s1_recv,
    g_send,
    g_recv,
    l_send,
    l_recv,
    b_send,
    b_recv,
    sum_send,
    sum_recv,
    rat_send,
    rat_recv,
    in_sem,
    own_sem,
):
    me = lax.axis_index("shard")
    t = lax.axis_index("tensor")
    sib = t + 1 - 2 * lax.rem(t, 2)
    across = lax.rem(t + 2, 4)
    diag = lax.rem(sib + 2, 4)
    blocks, rows, width = grad_ref.shape
    side = rows * shards
    slots = left.shape[0]
    main = width // 128 * 128
    tail = width - main
    wide = main + 128
    half = 2 * width
    low, high = half // 128 * 128, -(-half // 128) * 128
    y = t // 2
    out_bufs, owns = (out_0, out_1), (own_0, own_1)
    backs, ins = (back_0, back_1), (in_0, in_1)
    t_rows = pl.ds(pl.multiple_of(t * width, 32), width)
    across_rows = pl.ds(pl.multiple_of(across * width, 32), width)

    def peer(d):
        return lax.rem(me + d, shards)

    def strip(s):
        return pl.ds(pl.multiple_of(s * rows, 16), rows)

    root_in = [
        pltpu.make_async_copy(
            left_root_hbm.at[k], left_root.at[k, t_rows, :], in_sem.at[k]
        )
        for k in range(slots)
    ]
    stat_in = [
        pltpu.make_async_copy(src, dst, in_sem.at[slots + i])
        for i, (src, dst) in enumerate(
            ((moment_hbm, moment), (left_hbm, left), (right_hbm, right))
        )
    ]
    first_in = [
        pltpu.make_async_copy(src, dst, in_sem.at[slots + 3 + i])
        for i, (src, dst) in enumerate(
            ((owner_hbm, owner_ref), (grad_hbm, grad_ref), (right_root_hbm, right_root_ref))
        )
    ]
    for copy in first_in + root_in:
        copy.start()

    barrier = pltpu.get_barrier_semaphore()

    @pl.loop(1, shards)
    def _(d):
        pl.semaphore_signal(barrier, inc=1, device_id=(peer(d), t), device_id_type=MESH)

    for other in (sib, across, diag):
        pl.semaphore_signal(barrier, inc=1, device_id=(me, other), device_id_type=MESH)

    first_in[0].wait()

    owners = [owner_ref[b] for b in range(blocks)]
    slot_of = []
    for b in range(blocks):
        place = owners[b] * slots
        for c in range(b):
            place = place + jnp.where(owners[c] == owners[b], 1, 0)
        slot_of.append(place)

    def pick(k, s):
        source = jnp.int32(0)
        found = jnp.int32(0)
        for b in range(blocks):
            hit = slot_of[b] == s * slots + k
            source = jnp.where(hit, b, source)
            found = jnp.where(hit, 1, found)
        block = grad_ref[source]
        return jnp.where(found > 0, block, jnp.zeros_like(block))

    def shifted(count, lanes, shift):
        row = lax.broadcasted_iota(jnp.int32, (count, lanes), 0)
        col = lax.broadcasted_iota(jnp.int32, (count, lanes), 1)
        return (col == row + shift).astype(jnp.bfloat16)

    def pack(s):
        first, second = pick(0, s), pick(1, s)
        ends = mm(first[:, main:], shifted(tail, 128, 0), NN) + mm(
            second[:, main:], shifted(tail, 128, tail), NN
        )
        return first[:, :main], ends.astype(jnp.bfloat16), second[:, :main]

    first_in[1].wait()
    pl.semaphore_wait(barrier, shards - 1 + 3)

    def s1_copy(k, d):
        s = peer(d)
        return pltpu.make_async_remote_copy(
            src_ref=out_bufs[k].at[s],
            dst_ref=owns[k].at[strip(me), :],
            send_sem=s1_send.at[k, s],
            recv_sem=s1_recv.at[k, me],
            device_id=(s, t),
            device_id_type=MESH,
        )

    def s1_arrival(k, d):
        s = peer(d)
        return pltpu.make_async_remote_copy(
            src_ref=out_bufs[k].at[s],
            dst_ref=owns[k].at[strip(s), :],
            send_sem=s1_send.at[k, s],
            recv_sem=s1_recv.at[k, s],
            device_id=(s, t),
            device_id_type=MESH,
        )

    def panel_copy(buf, send, recv, k, panel, hop, target, lanes=slice(None)):
        return pltpu.make_async_remote_copy(
            src_ref=buf.at[k, panel, lanes],
            dst_ref=buf.at[k, panel, lanes],
            send_sem=send.at[k, hop],
            recv_sem=recv.at[k, hop],
            device_id=(me, target),
            device_id_type=MESH,
        )

    def window(which):
        return pl.ds(pl.multiple_of(low * which, 128), high)

    def mirror(k):
        root_moves[k][0].wait_recv()
        turn = shifted(half, high, (half - low) * (1 - y))

        @pl.loop(0, low // 256)
        def _(j):
            here = pl.ds(pl.multiple_of(high * y + 256 * j, 128), 256)
            there = pl.ds(pl.multiple_of(half * (1 - y), 32), half)
            piece = left_root[k, here, window(1 - y)]
            left_root[k, there, here] = mm(turn, piece, NT).astype(jnp.bfloat16)

    def root_copies(k):
        return (
            panel_copy(left_root, l_send, l_recv, k, t_rows, 0, sib),
            panel_copy(left_root, l_send, l_recv, k, t_rows, 1, across, window(y)),
            panel_copy(left_root, l_send, l_recv, k, across_rows, 2, sib, window(1 - y)),
        )

    def grad_copies(k):
        return (
            panel_copy(grad_t, g_send, g_recv, k, t_rows, 0, sib),
            panel_copy(grad_t, g_send, g_recv, k, t_rows, 1, across),
            panel_copy(grad_t, g_send, g_recv, k, across_rows, 2, sib),
        )

    root_moves = [root_copies(k) for k in range(slots)]
    grad_moves = [grad_copies(k) for k in range(slots)]

    @pl.loop(1, shards)
    def _(d):
        s = peer(d)
        first, ends, second = pack(s)
        out_0[s, :, 0:main] = first
        out_0[s, :, main:wide] = ends
        out_1[s] = second
        s1_copy(0, d).start()

    for k in range(slots):
        root_in[k].wait()
        root_moves[k][1].start()
        root_moves[k][0].start()

    @pl.loop(1, shards)
    def _(d):
        s1_copy(1, d).start()

    first, ends, second = pack(me)
    own_0[strip(me), 0:main] = first
    own_0[strip(me), main:wide] = ends
    own_1[strip(me), :] = second
    prod_t[1, width:, :] = jnp.zeros((wide - width, side), jnp.bfloat16)
    tail_t[...] = jnp.zeros((128, side), jnp.bfloat16)
    for copy in stat_in:
        copy.start()

    def turn_panel(k):
        @pl.loop(1, shards)
        def _(d):
            s1_arrival(k, d).wait_recv()

        for j in range(side // TILE):
            at = slice(j * TILE, (j + 1) * TILE)
            if k == 0:
                grad_t[0, t_rows, at] = mm(shifted(width, wide, 0), own_0[at, :], NT).astype(
                    jnp.bfloat16
                )
            else:
                top = pl.ds(pl.multiple_of(t * width, 32), main)
                end = pl.ds(pl.multiple_of(t * width + main, 32), tail)
                grad_t[1, top, at] = mm(shifted(main, main, 0), own_1[at, :], NT).astype(
                    jnp.bfloat16
                )
                grad_t[1, end, at] = mm(
                    shifted(tail, 128, tail), own_0[at, main:wide], NT
                ).astype(jnp.bfloat16)
        grad_moves[k][1].start()
        grad_moves[k][0].start()

    def pass_on(moves):
        moves[1].wait_recv()
        moves[2].start()

    chunk = 96

    def moments(k):
        def one(j, total):
            at = pl.ds(pl.multiple_of(j * chunk, 32), chunk)
            g = grad_t[k, pl.ds(pl.multiple_of(t * width + j * chunk, 32), chunk), :].astype(
                jnp.float32
            )
            fresh = moment_decay * moment[k, at, :] + (1.0 - moment_decay) * g * g
            moment[k, at, :] = fresh
            direction = g / jnp.sqrt(fresh)
            return total + jnp.sum(direction * direction, axis=0, keepdims=True)

        total = lax.fori_loop(0, width // chunk, one, jnp.zeros((1, side), jnp.float32))
        sums[t, 0, k] = jnp.full((8, 128), jnp.sum(total), jnp.float32)

    def back_copy(k, s):
        return pltpu.make_async_remote_copy(
            src_ref=backs[k].at[s],
            dst_ref=ins[k].at[me],
            send_sem=b_send.at[k, s],
            recv_sem=b_recv.at[k, me],
            device_id=(s, t),
            device_id_type=MESH,
        )

    own_copies = [
        pltpu.make_async_copy(backs[k].at[me], ins[k].at[me], own_sem.at[k]) for k in range(slots)
    ]

    def back_arrival(k, d):
        s = peer(d)
        return pltpu.make_async_remote_copy(
            src_ref=backs[k].at[s],
            dst_ref=ins[k].at[s],
            send_sem=b_send.at[k, s],
            recv_sem=b_recv.at[k, s],
            device_id=(s, t),
            device_id_type=MESH,
        )

    def precondition(k):
        @pl.loop(0, side // TILE)
        def _(j):
            at = pl.ds(pl.multiple_of(j * TILE, 128), TILE)
            prod_t[k, 0:width, at] = mm(right_root_ref[k], grad_t[k, :, at], NN).astype(
                jnp.bfloat16
            )

        if k == 0:
            tail_t[tail : 2 * tail, :] = prod_t[0, main:width, :]
        root_moves[k][2].wait_recv()

        group = shards // 2
        lanes = main if k == 0 else wide
        squares, end_squares = jnp.zeros((1, lanes), jnp.float32), jnp.zeros((1, 128), jnp.float32)
        for turn in range(2):
            first = lax.rem(me // group + 1 + turn, 2) * group
            band = pl.ds(pl.multiple_of(first * rows, 32), group * rows)
            part = mm(left_root[k, band, :], prod_t[k, 0:lanes, :], NT)
            squares += jnp.sum(part * part, axis=0, keepdims=True)
            if k == 1:
                ends = mm(left_root[0, band, :], tail_t[...], NT)
                end_squares += jnp.sum(ends * ends, axis=0, keepdims=True)
            for j in range(group):
                piece = part[j * rows : (j + 1) * rows]
                if k == 0:
                    back_0[first + j] = piece.astype(jnp.bfloat16)
                else:
                    back_1[first + j, :, 0:main] = piece[:, 0:main].astype(jnp.bfloat16)
                    back_1[first + j, :, main:wide] = (
                        piece[:, main:wide] + ends[j * rows : (j + 1) * rows]
                    ).astype(jnp.bfloat16)
        @pl.loop(1, shards)
        def _(d):
            back_copy(k, peer(d)).start()

        own_copies[k].start()
        total = (squares, end_squares)
        sums[t, 1, k] = jnp.full((8, 128), jnp.sum(total[0]), jnp.float32)
        if k == 1:
            sums[t, 1, 0] = sums[t, 1, 0] + jnp.full((8, 128), jnp.sum(total[1]), jnp.float32)

    start = pl.multiple_of(t * width // 128 * 128, 128)
    shift = t * width - start
    select = shifted(width, TILE, shift)

    def grams(k):
        rows_t = mm(select, grad_t[k, :, pl.ds(start, TILE)], NT).astype(jnp.bfloat16)

        @pl.loop(0, side // TILE)
        def _(j):
            at = pl.ds(pl.multiple_of(j * TILE, 128), TILE)
            left[k, :, at] = stat_decay * left[k, :, at] + mm(
                rows_t, grad_t[k, :, at], NN
            ) / MODEL_WIDTH
            right[k, :, at] = stat_decay * right[k, :, at] + mm(
                grad_t[k, t_rows, :], grad_t[k, at, :], NT
            ) / MODEL_WIDTH


    for k in range(slots):
        mirror(k)
    first_in[2].wait()
    turn_panel(0)
    for k in range(slots):
        pass_on(root_moves[k])
    for copy in stat_in:
        copy.wait()
    moments(0)
    turn_panel(1)

    for k in range(slots):
        pass_on(grad_moves[k])
        for hop in (0, 2):
            grad_moves[k][hop].wait_recv()
        precondition(k)
        if k + 1 < slots:
            moments(k + 1)
            grams(k)

    sum_moves = [
        pltpu.make_async_remote_copy(
            src_ref=sums.at[t],
            dst_ref=sums.at[t],
            send_sem=sum_send.at[i],
            recv_sem=sum_recv.at[i],
            device_id=(me, other),
            device_id_type=MESH,
        )
        for i, other in enumerate((sib, across, diag))
    ]
    for move in sum_moves:
        move.start()
    grams(slots - 1)
    for move in sum_moves:
        move.wait_recv()

    entries = float(MODEL_WIDTH * MODEL_WIDTH)
    totals = sums[0] + sums[1] + sums[2] + sums[3]
    ratio = jnp.sqrt(totals[0] / entries) / jnp.sqrt(totals[1] / entries + graft_eps)
    mine = pl.ds(me * slots, slots)
    ratios[mine] = ratio

    def ratio_copy(d):
        s = peer(d)
        return pltpu.make_async_remote_copy(
            src_ref=ratios.at[mine],
            dst_ref=ratios.at[mine],
            send_sem=rat_send.at[s],
            recv_sem=rat_recv.at[me],
            device_id=(s, t),
            device_id_type=MESH,
        )

    def ratio_arrival(d):
        s = peer(d)
        theirs = pl.ds(s * slots, slots)
        return pltpu.make_async_remote_copy(
            src_ref=ratios.at[theirs],
            dst_ref=ratios.at[theirs],
            send_sem=rat_send.at[s],
            recv_sem=rat_recv.at[s],
            device_id=(s, t),
            device_id_type=MESH,
        )

    @pl.loop(1, shards)
    def _(d):
        ratio_copy(d).start()

    @pl.loop(1, shards)
    def _(d):
        ratio_arrival(d).wait_recv()
        for k in range(slots):
            back_arrival(k, d).wait_recv()

    @pl.loop(1, shards)
    def _(d):
        ratio_copy(d).wait_send()
        for k in range(slots):
            s1_copy(k, d).wait_send()
            back_copy(k, peer(d)).wait_send()

    for k in range(slots):
        for move in root_moves[k] + grad_moves[k]:
            move.wait_send()
    for move in sum_moves:
        move.wait_send()
    for copy in own_copies:
        copy.wait()


def finish_kernel(
    owners,
    weights,
    first,
    second,
    ratios,
    left,
    right,
    moment,
    weights_out,
    left_out,
    right_out,
    moment_out,
    sem,
):
    copies = [
        pltpu.make_async_copy(src.at[k], dst.at[k], sem.at[i, k])
        for i, (src, dst) in enumerate(((left, left_out), (right, right_out), (moment, moment_out)))
        for k in range(src.shape[0])
    ]
    for copy in copies:
        copy.start()
    blocks, _, width = weights.shape
    main = first.shape[2]
    tail = width - main
    for b in range(blocks):
        rank = jnp.int32(0)
        for c in range(b):
            rank = rank + jnp.where(owners[c] == owners[b], 1, 0)
        scale = -learn_rate * ratios[owners[b] * SLOTS + rank][0:1, 0:1]
        other = second[owners[b]]
        whole = jnp.where(rank == 0, first[owners[b]], other[:, 0:main]).astype(jnp.float32)
        ends = other[:, main:].astype(jnp.float32)
        ends = jnp.where(rank == 0, ends[:, tail : 2 * tail], ends[:, 0:tail])
        weights_out[b, :, 0:main] = weights[b, :, 0:main] + scale * whole
        weights_out[b, :, main:] = weights[b, :, main:] + scale * ends
    for copy in copies:
        copy.wait()


def kernel_body(
    gradients,
    weights,
    owner_list,
    left_gram_stats,
    right_gram_stats,
    left_root,
    right_root,
    adam_second_moment,
):
    shards = lax.axis_size("shard")
    blocks, rows, width = gradients.shape
    slots = left_gram_stats.shape[0]
    side = rows * shards
    main = width // 128 * 128
    wide = main + 128
    bf16, f32 = jnp.bfloat16, jnp.float32
    flip = lambda a: jnp.transpose(a, (0, 2, 1))
    hbm = pl.BlockSpec(memory_space=pl.ANY)
    vmem = pl.BlockSpec(memory_space=pltpu.VMEM)
    dma = lambda *shape: pltpu.SemaphoreType.DMA(shape)
    stat = jax.ShapeDtypeStruct((slots, width, side), f32)
    first, second, ratios, new_left, new_right, new_moment = pl.pallas_call(
        functools.partial(step_kernel, shards),
        out_shape=(
            jax.ShapeDtypeStruct((shards, rows, main), bf16),
            jax.ShapeDtypeStruct((shards, rows, wide), bf16),
            jax.ShapeDtypeStruct((slots * shards, 8, 128), f32),
            stat,
            stat,
            stat,
        ),
        in_specs=[pl.BlockSpec(memory_space=pltpu.HBM)] * 7,
        out_specs=(hbm, hbm, vmem, vmem, vmem, vmem),
        scratch_shapes=[
            pltpu.VMEM((shards, rows, wide), bf16),
            pltpu.VMEM((shards, rows, main), bf16),
            pltpu.VMEM((side, wide), bf16),
            pltpu.VMEM((side, main), bf16),
            pltpu.VMEM((slots, side, side), bf16),
            pltpu.VMEM((slots, side, side), bf16),
            pltpu.VMEM((slots, wide, side), bf16),
            pltpu.VMEM((128, side), bf16),
            pltpu.VMEM((shards, rows, main), bf16),
            pltpu.VMEM((shards, rows, wide), bf16),
            pltpu.VMEM((4, 2, slots, 8, 128), f32),
            pltpu.SMEM((blocks,), jnp.int32),
            pltpu.VMEM((blocks, rows, width), bf16),
            pltpu.VMEM((slots, width, side), bf16),
            dma(slots, shards),
            dma(slots, shards),
            dma(slots, 3),
            dma(slots, 3),
            dma(slots, 3),
            dma(slots, 3),
            dma(slots, shards),
            dma(slots, shards),
            dma(3),
            dma(3),
            dma(shards),
            dma(shards),
            dma(slots + 6),
            dma(slots),
        ],
        compiler_params=pltpu.CompilerParams(
            collective_id=0, has_side_effects=True, vmem_limit_bytes=40 * 2**20
        ),
    )(
        owner_list,
        gradients,
        flip(right_root),
        flip(left_root),
        left_gram_stats,
        right_gram_stats,
        flip(adam_second_moment),
    )
    new_weights, new_left, new_right, new_moment = pl.pallas_call(
        finish_kernel,
        in_specs=[pl.BlockSpec(memory_space=pltpu.SMEM)] + [vmem] * 7,
        out_specs=(vmem, hbm, hbm, hbm),
        out_shape=(jax.ShapeDtypeStruct((blocks, rows, width), f32), stat, stat, stat),
        scratch_shapes=[dma(3, slots)],
        compiler_params=pltpu.CompilerParams(vmem_limit_bytes=24 * 2**20),
    )(owner_list, weights, first, second, ratios, new_left, new_right, new_moment)
    return (new_weights, new_left, new_right, flip(new_moment))


def fits(mesh, gradients, slot_total):
    shards, tensor = mesh.shape["shard"], mesh.shape["tensor"]
    blocks, side, _ = gradients.shape
    rows, width = side // shards, side // tensor
    slots = slot_total // shards
    part = slots * width // blocks
    return (
        tensor == 4
        and slots == 2
        and rows % 16 == 0
        and shards % 2 == 0
        and rows * shards // 2 % 32 == 0
        and width % 96 == 0
        and width <= TILE - 96
        and 0 < width % 128 <= 64
        and side % TILE == 0
        and (side // 2) // 128 * 128 % 256 == 0
        and part % 8 == 0
        and width % part == 0
    )


def solution(mesh):
    def run(gradients, *others):
        chosen = kernel_body if fits(mesh, gradients, others[2].shape[0]) else body
        return mapped(chosen)(gradients, *others)

    mapped = lambda chosen: jax.shard_map(
        chosen,
        mesh=mesh,
        in_specs=(
            P(None, "shard", "tensor"),
            P(None, "shard", "tensor"),
            P(),
            P("shard", "tensor", None),
            P("shard", "tensor", None),
            P("shard", None, "tensor"),
            P("shard", None, "tensor"),
            P("shard", None, "tensor"),
        ),
        out_specs=(
            P(None, "shard", "tensor"),
            P("shard", "tensor", None),
            P("shard", "tensor", None),
            P("shard", None, "tensor"),
        ),
        check_vma=False,
    )
    return run
```
